512 devices in a mesh: tm: 8 (over z_lo, core), gz: 64 (over x, z_hi, y).
Axes of the slice: x: 4, y: 8, z: 8 (z_hi: 2, z_lo: 4; z = z_hi * 4 + z_lo), core: 2. Of those that a mesh axis runs over, the one named last changes fastest.
Arguments:
- init_states: float32 [8, 2, 128, 32, 256], P('tm', None, 'gz'), may hold values from 0 to 1
- diffusivity: float32 [128, 32, 256], P('gz'), may hold values from 0.5 to 2
Outputs:
- nodes: float32 [8, 3, 2, 128, 32, 256], P('tm', None, None, 'gz')
The draws below stay inside these ranges and needn't reach their ends.
All inputs are finite; a program needn't handle non-finite values.
Results may differ from the reference program's by a relative error of at most 0.0001.
Values sent between devices are 32-bit elements; how exact they have to be, the bound alone decides.
A program may use at most 64 MiB of HBM per device.

```python
import math
import jax
import jax.numpy as jnp

X = 32
Y = 256
NT = 8
NZ = 128


def level_of(stream_key, dims, cuts, least, top_value):
    def one(position, shards_of):
        draws = jax.random.uniform(jax.random.fold_in(jax.random.fold_in(stream_key, 6), position), (shards_of,), jnp.float32, least / len(cuts), top_value / len(cuts))
        return jnp.repeat(jnp.exp(draws), dims[position] // shards_of).reshape((-1,) + (1,) * (len(dims) - position - 1))

    loudness = one(*cuts[0])
    for cut in cuts[1:]:
        loudness = loudness * one(*cut)
    return loudness


def setup_inputs(seed: int = 0) -> dict:
    seeds = jax.random.split(jax.random.key(seed), 3)
    return {
        "init_states": jnp.clip(1.0 * jax.random.uniform(seeds[0], (NT, 2, NZ, X, Y), jnp.float32) ** level_of(seeds[0], (NT, 2, NZ, X, Y), ((0, 8), (2, 64)), -0.2, 0.2), 0.0, 1.0),
        "diffusivity": jnp.clip(jnp.exp(math.log(2.0) - 1.3862944 * jax.random.uniform(seeds[1], (NZ, X, Y), jnp.float32) ** level_of(seeds[1], (NZ, X, Y), ((0, 64),), -0.2, 0.2)), 0.5, 2.0),
    }


DIFF_U = 0.16
DIFF_V = 0.08
FEED_RATE = 0.035
KILL_RATE = 0.06
TIME_STEP = 0.8
HALF_STEP = 0.4
WEIGHTS = ((5.0 / 24.0, 1.0 / 3.0, -1.0 / 24.0), (-1.0 / 24.0, 1.0 / 3.0, 5.0 / 24.0))


def laplace_pad(padded, spacing):
    centre = padded[:, :, 1:-1]
    along_z = padded[:, :, 2:] + padded[:, :, :-2] - 2.0 * centre
    along_x = jnp.roll(centre, 1, 3) + jnp.roll(centre, -1, 3) - 2.0 * centre
    along_y = jnp.roll(centre, 1, 4) + jnp.roll(centre, -1, 4) - 2.0 * centre
    return centre, along_z + (along_x + along_y) / spacing


def reaction(padded, diffuse, spacing):
    centre, laplace = laplace_pad(padded, spacing)
    conc_u = centre[:, 0]
    conc_v = centre[:, 1]
    product = conc_u * conc_v * conc_v
    rate_u = DIFF_U * diffuse * laplace[:, 0] - product + FEED_RATE * (1.0 - conc_u)
    rate_v = DIFF_V * diffuse * laplace[:, 1] + product - (FEED_RATE + KILL_RATE) * conc_v
    return jnp.stack([rate_u, rate_v], 1)


def integral(rates, row):
    return TIME_STEP * (WEIGHTS[row][0] * rates[0] + WEIGHTS[row][1] * rates[1] + WEIGHTS[row][2] * rates[2])


def coarsen(field):
    shape = field.shape[:-2] + (field.shape[-2] // 2, 2, field.shape[-1] // 2, 2)
    return 0.25 * jnp.sum(field.reshape(shape), axis=(-3, -1))


def refine(field):
    return jnp.repeat(jnp.repeat(field, 2, -2), 2, -1)


def sweep(begin, first_rate, old_rates, consts, evaluate):
    u_one = begin + HALF_STEP * (first_rate - old_rates[0]) + consts[0]
    rate_one = evaluate(u_one)
    u_two = u_one + HALF_STEP * (rate_one - old_rates[1]) + consts[1]
    return u_one, rate_one, u_two


def wrap_pad(state):
    return jnp.concatenate([state[:, -1:], state, state[:, :1]], axis=1)[None]


def reference(init_states, diffusivity):
    slices = init_states.shape[0]
    coarse_diff = coarsen(diffusivity)

    def fine_rate(state):
        return reaction(wrap_pad(state), diffusivity, 1.0)[0]

    def coarse_rate(state):
        return reaction(wrap_pad(state), coarse_diff, 4.0)[0]

    provisional = []
    coarse_old = []
    coarse_rates = []
    coarse_consts = []
    for index in range(slices):
        initial = init_states[index]
        rate_init = fine_rate(initial)
        same = (rate_init, rate_init, rate_init)
        consts = (integral(same, 0), integral(same, 1))
        u_one, rate_one, u_two = sweep(initial, rate_init, same, consts, fine_rate)
        rate_two = fine_rate(u_two)
        nodes_a = (initial, u_one, u_two)
        rates_a = (rate_init, rate_one, rate_two)
        coarse_nodes = tuple(coarsen(item) for item in nodes_a)
        provisional.append(nodes_a)
        coarse_old.append(coarse_nodes)
        coarse_rates.append(tuple(coarse_rate(item) for item in coarse_nodes))
        coarse_consts.append((coarsen(integral(rates_a, 0)), coarsen(integral(rates_a, 1))))
    corrected = []
    begin = coarse_old[0][0]
    for index in range(slices):
        c_one, rate_skip, c_two = sweep(begin, coarse_rate(begin), coarse_rates[index], coarse_consts[index], coarse_rate)
        new_nodes = (begin, c_one, c_two)
        corrected.append(tuple(provisional[index][node] + refine(new_nodes[node] - coarse_old[index][node]) for node in range(3)))
        begin = c_two
    outputs = []
    for index in range(slices):
        nodes_c = corrected[index]
        begin = nodes_c[0] if index == 0 else corrected[index - 1][2]
        old_rates = tuple(fine_rate(item) for item in nodes_c)
        consts = (integral(old_rates, 0), integral(old_rates, 1))
        u_one, rate_skip, u_two = sweep(begin, fine_rate(begin), old_rates, consts, fine_rate)
        outputs.append(jnp.stack([begin, u_one, u_two]))
    return jnp.stack(outputs)
```

```python
import jax
import jax.numpy as jnp
from jax import lax
from jax.experimental import pallas as pl
from jax.experimental.pallas import tpu as pltpu
from jax.sharding import PartitionSpec as P


MESH = pl.DeviceIdType.MESH
F32 = jnp.float32
STEP = 0.4
W_ONE = (0.8 * 5.0 / 24.0, 0.8 / 3.0, -0.8 / 24.0)
W_TWO = (-0.8 / 24.0, 0.8 / 3.0, 0.8 * 5.0 / 24.0)

CONSTS = (
    (0, 0, 6), (1, 0, 4), (2, 0, 2), (3, 0, 0), (3, 3, 2), (4, 7, 8), (5, 7, 6), (6, 7, 4), (7, 7, 2), (4, 5, 4), (5, 5, 2),
)
WIDTHS = (8, 6, 4, 2, 0)
RUNS = {8: (7,), 6: (0, 7), 4: (0, 5, 7), 2: (0, 3, 5, 7), 0: (0,)}
COARSE_REACH = {0: 3, 3: 2, 5: 3, 7: 5}
MID = 10


def span(k):
    return [0] + [s * i for i in range(1, k + 1) for s in (1, -1)]


def sides(k):
    return span(k)[1:]


def pairs():
    out = set()
    for t in range(8):
        out |= {(t, t, j) for j in sides(2)}
        if t:
            out |= {(t - 1, t, j) for j in span(1)}
    for t, reach in COARSE_REACH.items():
        out |= {(t, t, j) for j in sides(reach)}
    for src, dst, h in CONSTS:
        out |= {(src, dst, j) for j in span(h // 2 + 1) if src != dst or j}
    out |= {(0, 3, j) for j in span(2)} | {(0, 5, j) for j in span(3)} | {(0, 7, j) for j in span(5)}
    out |= {(0, 1, 0), (0, 2, 0), (5, 4, 0), (7, 6, 0)}
    return sorted(out)


def get(ref, *at):
    return [[ref[(*at, s, p)] for p in range(4)] for s in range(2)]


def get_coarse(ref, *at):
    return [ref[(*at, s)] for s in range(2)]


def react(u, v, lap_u, lap_v, du):
    uvv = u * v * v
    return du * lap_u - uvv + 0.035 * (1.0 - u), (0.5 * du) * lap_v + uvv - 0.095 * v


def fine_rate(low, mid, high, du):
    laps = []
    for s in range(2):
        row = []
        for p in range(4):
            across = mid[s][p ^ 2]
            along = mid[s][p ^ 1]
            xs = across + pltpu.roll(across, 15 if p & 2 else 1, 0)
            ys = along + pltpu.roll(along, 127 if p & 1 else 1, 1)
            row.append((low[s][p] + high[s][p]) + (xs + ys) - 6.0 * mid[s][p])
        laps.append(row)
    both = [react(mid[0][p], mid[1][p], laps[0][p], laps[1][p], du[p]) for p in range(4)]
    return [[b[s] for b in both] for s in range(2)]


def coarse_rate(low, mid, high, du):
    laps = []
    for s in range(2):
        c = mid[s]
        xs = pltpu.roll(c, 1, 0) + pltpu.roll(c, 15, 0)
        ys = pltpu.roll(c, 1, 1) + pltpu.roll(c, 127, 1)
        laps.append((low[s] + high[s]) + 0.25 * (xs + ys) - 3.0 * c)
    return react(mid[0], mid[1], laps[0], laps[1], du)


def average(parts):
    return 0.25 * ((parts[0] + parts[1]) + (parts[2] + parts[3]))


def loop(count, body, chunk=1):
    def many(k, carry):
        for i in range(chunk):
            body(k * chunk + i)
        return carry

    lax.fori_loop(0, count // chunk, many, 0)


def swap(forward):
    rows = lax.broadcasted_iota(jnp.int32, (256, 256), 0)
    cols = lax.broadcasted_iota(jnp.int32, (256, 256), 1)
    if not forward:
        rows, cols = cols, rows
    return jnp.where(rows == 2 * (cols % 128) + cols // 128, 1.0, 0.0).astype(F32)


def kernel(
    init, diff, out, xin, din, tmp, woven, a0, a1, a2, ap, du, cd, v0, v1, r0, r1, r2, own, base, one, two,
    d8, d6, d4, d2, d0, b10, b8, b6, b4, b2, b0, w8, w6, w4, w2, w0, dummy,
    in_sem, near_s, near_r, cd_s, cd_r, far_s, far_r, prev_s, prev_r, const_s, const_r, state_s, state_r, give_s, give_r,
):
    tm = lax.axis_index("tm")
    gz = lax.axis_index("gz")
    count = lax.axis_size("gz")
    const = {8: d8, 6: d6, 4: d4, 2: d2, 0: d0}
    state = {10: b10, 8: b8, 6: b6, 4: b4, 2: b2, 0: b0}
    middle = {8: w8, 6: w6, 4: w4, 2: w2, 0: w0}

    def at(t, j):
        return {"tm": t, "gz": lax.rem(gz + (j + count), count)}

    def send(src, dst, ssem, rsem, t, j):
        pltpu.make_async_remote_copy(
            src_ref=src, dst_ref=dst, send_sem=ssem, recv_sem=rsem, device_id=at(t, j), device_id_type=MESH
        ).start()

    def wait(sem, units):
        ref = dummy.at[pl.ds(0, units)]
        pltpu.make_async_copy(ref, ref, sem).wait()

    def on(*slices):
        cond = tm == slices[0]
        for t in slices[1:]:
            cond = cond | (tm == t)
        return pl.when(cond)

    load_x = pltpu.make_async_copy(init.at[0], xin, in_sem.at[0])
    load_d = pltpu.make_async_copy(diff, din, in_sem.at[1])
    load_x.start()
    load_d.start()
    barrier = pltpu.get_barrier_semaphore()
    met = pairs()
    for t in range(8):
        @on(t)
        def _(t=t):
            for src, dst, j in met:
                if dst == t:
                    pl.semaphore_signal(barrier, inc=1, device_id=at(src, -j), device_id_type=MESH)

    order = swap(True)
    load_x.wait()
    load_d.wait()

    def split(rows):
        return jnp.dot(rows, order, precision=lax.Precision.HIGHEST, preferred_element_type=F32)

    mixed = split(xin[...].reshape(128, 256)).reshape(4, 32, 256)
    mixed_d = split(din[...].reshape(64, 256)).reshape(2, 32, 256)
    for half in range(2):
        tmp[half, 0:4] = mixed[:, :, half * 128 : half * 128 + 128]
        tmp[half, 4:6] = mixed_d[:, :, half * 128 : half * 128 + 128]
    for layer in range(2):
        for p in range(4):
            rows = pl.ds(p // 2, 16, stride=2)
            for s in range(2):
                a0[3 + layer, s, p] = tmp[p % 2, s * 2 + layer, rows, :]
            du[2 + layer, p] = 0.16 * tmp[p % 2, 4 + layer, rows, :]
        cd[MID + layer] = average([du[2 + layer, p] for p in range(4)])

    greetings = sum(jnp.where(tm == t, sum(src == t for src, _, _ in met), 0) for t in range(8))
    pl.semaphore_wait(barrier, greetings)

    two_own = pl.ds(3, 2)
    send(a0.at[two_own], a0.at[pl.ds(1, 2)], near_s, near_r, tm, 1)
    send(a0.at[two_own], a0.at[pl.ds(5, 2)], near_s, near_r, tm, -1)
    send(a0.at[4], a0.at[0], near_s, near_r, tm, 2)
    send(a0.at[3], a0.at[7], near_s, near_r, tm, -2)
    send(du.at[pl.ds(2, 2)], du.at[pl.ds(0, 2)], near_s, near_r, tm, 1)
    send(du.at[pl.ds(2, 2)], du.at[pl.ds(4, 2)], near_s, near_r, tm, -1)
    for t, reach in COARSE_REACH.items():
        @on(t)
        def _(t=t, reach=reach):
            for j in sides(reach):
                send(cd.at[pl.ds(MID, 2)], cd.at[pl.ds(MID - 2 * j, 2)], cd_s, cd_r, t, j)
    wait(near_r, 32)

    def first(i):
        c = get(a0, i + 1)
        f = fine_rate(get(a0, i), c, get(a0, i + 2), [du[i, p] for p in range(4)])
        for s in range(2):
            for p in range(4):
                a1[i, s, p] = c[s][p] + STEP * f[s][p]
            r0[i, s] = average(f[s])
            v0[i, s] = average(c[s])

    loop(6, first)

    def second(i):
        c = get(a1, i + 1)
        f = fine_rate(get(a1, i), c, get(a1, i + 2), [du[i + 1, p] for p in range(4)])
        for s in range(2):
            for p in range(4):
                a2[i + 1, s, p] = c[s][p] + STEP * f[s][p]
            r1[i, s] = average(f[s])
            v1[i + 1, s] = average(c[s])

    loop(4, second)

    def third(i):
        f = fine_rate(get(a2, i + 1), get(a2, i + 2), get(a2, i + 3), [du[i + 2, p] for p in range(4)])
        for s in range(2):
            r2[i, s] = average(f[s])

    loop(2, third)

    is_first = jnp.where(tm == 0, 1.0, 0.0).astype(F32)
    for i in range(2):
        g_zero = coarse_rate(get_coarse(v0, i + 1), get_coarse(v0, i + 2), get_coarse(v0, i + 3), cd[MID + i])
        g_one = coarse_rate(get_coarse(v1, i + 1), get_coarse(v1, i + 2), get_coarse(v1, i + 3), cd[MID + i])
        for s in range(2):
            rates = (r0[i + 2, s], r1[i + 1, s], r2[i, s])
            c_zero = W_ONE[0] * rates[0] + W_ONE[1] * rates[1] + W_ONE[2] * rates[2]
            c_one = W_TWO[0] * rates[0] + W_TWO[1] * rates[1] + W_TWO[2] * rates[2]
            own[i, 0, s] = c_zero + is_first * v0[i + 2, s] - (1.0 - is_first) * (STEP * g_zero[s])
            own[i, 1, s] = c_one - STEP * g_one[s]

    for k, (src, dst, h) in enumerate(CONSTS):
        @on(src)
        def _(k=k, src=src, dst=dst, h=h):
            ref = const[h]
            sems = (const_s.at[k], const_r.at[h // 2])
            for j in reversed(span(h // 2)):
                here = pl.ds(h + 1 - 2 * j, 2)
                if src == dst and j == 0:
                    ref[here] = own[...]
                else:
                    send(own, ref.at[here], *sems, dst, j)
            j = h // 2 + 1
            send(own.at[1, 0], ref.at[0, 0], *sems, dst, j)
            send(own.at[0, 0], ref.at[2 * h + 3, 0], *sems, dst, -j)

    send(a2.at[2], a2.at[0], far_s, far_r, tm, 1)
    send(a2.at[3], a2.at[5], far_s, far_r, tm, -1)

    @pl.when(tm < 7)
    def _():
        for j in span(1):
            send(a2.at[pl.ds(2, 2)], ap.at[pl.ds(2 - 2 * j, 2)], prev_s, prev_r, tm + 1, j)

    def prepare():
        wait(far_r, 8)

        @pl.when(tm > 0)
        def _():
            wait(prev_r, 24)

        def body(i):
            for k, (ref, shift) in enumerate(((a0, 1), (a1, 0), (a2, 0), (ap, 0))):
                c = get(ref, i + shift)
                for s in range(2):
                    v = average(c[s])
                    for p in range(4):
                        base[k, i, s, p] = c[s][p] - v

        def body_first(i):
            for k, (ref, shift) in enumerate(((a0, 1), (a1, 0), (a2, 0))):
                c = get(ref, i + shift)
                for s in range(2):
                    v = average(c[s])
                    for p in range(4):
                        base[k, i, s, p] = c[s][p] - v

        @pl.when(tm > 0)
        def _():
            loop(6, body)

        @pl.when(tm == 0)
        def _():
            loop(6, body_first)

    @pl.when(tm > 0)
    def _():
        prepare()

    for t, reach in COARSE_REACH.items():
        @on(t)
        def _(reach=reach):
            wait(cd_r, 2 * reach)

    @on(3)
    def _():
        wait(state_r, 10)

    @on(5)
    def _():
        wait(state_r, 14)

    @on(7)
    def _():
        wait(state_r, 22)

    chunks = {20: 4, 18: 6, 16: 4, 14: 7, 12: 4, 10: 5, 8: 4, 6: 6, 4: 4, 2: 2}

    for h in WIDTHS:
        begin, mid, end, e = state[h + 2], middle[h], state[h], const[h]

        @on(*RUNS[h])
        def _(h=h, begin=begin, mid=mid, end=end, e=e):
            for src, dst, width in CONSTS:
                if width == h:
                    @on(dst)
                    def _(src=src, dst=dst):
                        wait(const_r.at[h // 2], 4 * h + 6 - (4 if src == dst else 0))

            def half(i):
                g = coarse_rate(get_coarse(begin, i), get_coarse(begin, i + 1), get_coarse(begin, i + 2), cd[MID + i - h - 1])
                for s in range(2):
                    mid[i, s] = begin[i + 1, s] + STEP * g[s] + e[i, 0, s]

            def given(i):
                for s in range(2):
                    mid[i, s] = e[i, 0, s]

            def full(i):
                g = coarse_rate(get_coarse(mid, i), get_coarse(mid, i + 1), get_coarse(mid, i + 2), cd[MID + i - h])
                for s in range(2):
                    end[i, s] = mid[i + 1, s] + STEP * g[s] + e[i + 1, 1, s]

            if h == 6:
                @pl.when(tm == 0)
                def _():
                    loop(2 * h + 4, given, 4)

                @pl.when(tm > 0)
                def _():
                    loop(2 * h + 4, half, chunks[2 * h + 4])
            else:
                loop(2 * h + 4, half, chunks[2 * h + 4])
            loop(2 * h + 2, full, chunks[2 * h + 2])

        def give(dst):
            for k, (src_ref, start, dst_ref, to) in enumerate(
                ((state[h + 2], h, b4, 2), (middle[h], h - 1, w2, 1), (state[h], h - 2, b2, 0))
            ):
                send(src_ref.at[pl.ds(start, 6)], dst_ref.at[pl.ds(to, 6)], give_s, give_r, dst, 0)

        if h == 4:
            @on(0)
            def _():
                give(1)

            @on(5, 7)
            def _():
                give(tm - 1)

        if h == 2:
            @on(0)
            def _():
                for j in span(2):
                    send(b2.at[pl.ds(2, 2)], b4.at[pl.ds(4 - 2 * j, 2)], state_s, state_r, 3, j)

        if h == 0:
            @on(0)
            def _():
                for j in reversed(span(5)):
                    send(b0, b10.at[pl.ds(10 - 2 * j, 2)], state_s, state_r, 7, j)
                for j in reversed(span(3)):
                    send(b0, b6.at[pl.ds(6 - 2 * j, 2)], state_s, state_r, 5, j)
                wait(give_s, 18)
                for src_ref, start in ((b4, 2), (w2, 1), (b2, 0)):
                    send(src_ref.at[pl.ds(start, 6)], src_ref.at[pl.ds(start, 6)], give_s, give_r, 2, 0)

    @pl.when(tm == 0)
    def _():
        prepare()

    @on(1, 2, 4, 6)
    def _():
        wait(give_r, 18)

    def correct(zero, zero_at, one_ref, one_at, two_ref, two_at, start):
        def body(i):
            for k, (ref, shift) in enumerate(((zero, zero_at), (one_ref, one_at), (two_ref, two_at))):
                for s in range(2):
                    w = ref[i + shift, s]
                    for p in range(4):
                        base[k, i, s, p] = base[k, i, s, p] + w
                        if k == 0:
                            if start:
                                base[3, i, s, p] = a0[i + 1, s, p]
                            else:
                                base[3, i, s, p] = base[3, i, s, p] + w

        loop(6, body)

    @pl.when(tm == 0)
    def _():
        correct(v0, 0, w6, 5, b6, 4, True)

    @pl.when(tm > 0)
    def _():
        correct(b4, 2, w2, 1, b2, 0, False)

    def fourth(i):
        d = [du[i + 1, p] for p in range(4)]
        f = [fine_rate(get(base, k, i), get(base, k, i + 1), get(base, k, i + 2), d) for k in range(4)]
        for s in range(2):
            for p in range(4):
                rates = [f[k][s][p] for k in range(3)]
                i_one = W_ONE[0] * rates[0] + W_ONE[1] * rates[1] + W_ONE[2] * rates[2]
                i_two = W_TWO[0] * rates[0] + W_TWO[1] * rates[1] + W_TWO[2] * rates[2]
                b_one = base[3, i + 1, s, p] + STEP * (f[3][s][p] - rates[0]) + i_one
                one[i, s, p] = b_one
                two[i, s, p] = b_one - STEP * rates[1] + i_two

    loop(4, fourth)

    def fifth(i):
        f = fine_rate(get(one, i), get(one, i + 1), get(one, i + 2), [du[i + 2, p] for p in range(4)])
        for s in range(2):
            for p in range(4):
                two[i + 1, s, p] = two[i + 1, s, p] + STEP * f[s][p]

    loop(2, fifth)

    back = swap(False)
    for node, (ref, shift) in enumerate(((base.at[3], 2), (one, 1), (two, 1))):
        rows = []
        for s in range(2):
            for layer in range(2):
                for half in range(2):
                    rows.append(
                        jnp.concatenate([ref[shift + layer, s, 2 * half], ref[shift + layer, s, 2 * half + 1]], axis=1)
                    )
        whole = jnp.dot(jnp.concatenate(rows, 0), back, precision=lax.Precision.HIGHEST, preferred_element_type=F32)
        for s in range(2):
            for layer in range(2):
                for side in range(2):
                    lanes = slice(side * 128, side * 128 + 128)
                    for half in range(2):
                        k = (s * 2 + layer) * 2 + half
                        woven[node, s, layer, side, pl.ds(half, 16, stride=2), :] = whole[k * 16 : k * 16 + 16, lanes]
                    out[0, node, s, layer, :, lanes] = woven[node, s, layer, side]

    wait(near_s, 32)
    wait(far_s, 8)
    for t, reach in COARSE_REACH.items():
        @on(t)
        def _(reach=reach):
            wait(cd_s, 2 * reach)

    @pl.when(tm < 7)
    def _():
        wait(prev_s, 24)

    for k, (src, dst, h) in enumerate(CONSTS):
        @on(src)
        def _(k=k, src=src, dst=dst, h=h):
            wait(const_s.at[k], 4 * h + 6 - (4 if src == dst else 0))

    @on(0)
    def _():
        wait(state_s, 46)

    @on(0, 5, 7)
    def _():
        wait(give_s, 18)


def local(init_states, diffusivity):
    fine = (2, 4, 16, 128)
    coarse = (2, 16, 128)

    def vm(*shape):
        return pltpu.VMEM(shape, F32)

    scratch = [vm(2, 2, 32, 256), vm(2, 32, 256), vm(2, 6, 32, 128), vm(3, 2, 2, 2, 32, 128)]
    scratch += [vm(8, *fine), vm(6, *fine), vm(6, *fine), vm(6, *fine), vm(6, 4, 16, 128), vm(2 * MID + 2, 16, 128)]
    scratch += [vm(6, *coarse), vm(6, *coarse), vm(6, *coarse), vm(4, *coarse), vm(2, *coarse), vm(2, 2, *coarse)]
    scratch += [vm(4, 6, *fine), vm(4, *fine), vm(4, *fine)]
    scratch += [vm(2 * h + 4, 2, *coarse) for h in WIDTHS]
    scratch += [vm(2 * h + 2, *coarse) for h in (10,) + WIDTHS]
    scratch += [vm(2 * h + 4, *coarse) for h in WIDTHS]
    scratch += [vm(48, *coarse)]
    dma = pltpu.SemaphoreType.DMA
    one = [dma(()), dma(())]
    scratch += [dma((2,))] + one * 4 + [dma((len(CONSTS),)), dma((5,))] + one * 2
    return pl.pallas_call(
        kernel,
        out_shape=jax.ShapeDtypeStruct((1, 3, 2, 2, 32, 256), F32),
        in_specs=[pl.BlockSpec(memory_space=pl.ANY)] * 2,
        out_specs=pl.BlockSpec(memory_space=pltpu.VMEM),
        scratch_shapes=scratch,
        name="pfasst",
        compiler_params=pltpu.CompilerParams(
            collective_id=0, has_side_effects=True, vmem_limit_bytes=32 * 1024 * 1024
        ),
    )(init_states, diffusivity)


def solution(mesh):
    placed = (P("tm", None, "gz", None, None), P("gz", None, None))
    return jax.shard_map(
        local,
        mesh=mesh,
        in_specs=placed,
        out_specs=P("tm", None, None, "gz", None, None),
        check_vma=False,
    )
```

```python
import jax
import jax.numpy as jnp
from jax import lax
from jax.experimental import pallas as pl
from jax.experimental.pallas import tpu as pltpu
from jax.sharding import PartitionSpec as P


MESH = pl.DeviceIdType.MESH
F32 = jnp.float32
STEP = 0.4
W_ONE = (0.8 * 5.0 / 24.0, 0.8 / 3.0, -0.8 / 24.0)
W_TWO = (-0.8 / 24.0, 0.8 / 3.0, 0.8 * 5.0 / 24.0)

CONSTS = (
    (0, 0, 6), (1, 0, 4), (2, 0, 2), (3, 0, 0), (3, 3, 2), (4, 7, 8), (5, 7, 6), (6, 7, 4), (7, 7, 2), (4, 5, 4), (5, 5, 2),
)
WIDTHS = (8, 6, 4, 2, 0)
RUNS = {8: (7,), 6: (0, 7), 4: (0, 5, 7), 2: (0, 3, 5, 7), 0: (0,)}
COARSE_REACH = {0: 3, 3: 2, 5: 3, 7: 5}
MID = 10


def span(k):
    return [0] + [s * i for i in range(1, k + 1) for s in (1, -1)]


def sides(k):
    return span(k)[1:]


def pairs():
    out = set()
    for t in range(8):
        out |= {(t, t, j) for j in sides(1)}
        out.add((t, t ^ 1, 0))
        if t:
            out.add((t - 1, t, 0))
    for t, reach in COARSE_REACH.items():
        out |= {(t, t, j) for j in sides(reach) if abs(j) > 1}
    for src, dst, h in CONSTS:
        out |= {(src, dst, j) for j in span(h // 2 + 1) if src != dst or j}
    out |= {(0, 3, j) for j in span(2)} | {(0, 5, j) for j in span(3)} | {(0, 7, j) for j in span(5)}
    out |= {(0, 1, 0), (0, 2, 0), (5, 4, 0), (7, 6, 0)}
    return sorted(out)


def get(ref, *at):
    return [[ref[(*at, s, p)] for p in range(4)] for s in range(2)]


def get_coarse(ref, *at):
    return [ref[(*at, s)] for s in range(2)]


def react(u, v, lap_u, lap_v, du):
    uvv = u * v * v
    return du * lap_u - uvv + 0.035 * (1.0 - u), (0.5 * du) * lap_v + uvv - 0.095 * v


def fine_rate(low, mid, high, du):
    laps = []
    for s in range(2):
        row = []
        for p in range(4):
            across = mid[s][p ^ 2]
            along = mid[s][p ^ 1]
            xs = across + pltpu.roll(across, 15 if p & 2 else 1, 0)
            ys = along + pltpu.roll(along, 127 if p & 1 else 1, 1)
            row.append((low[s][p] + high[s][p]) + (xs + ys) - 6.0 * mid[s][p])
        laps.append(row)
    both = [react(mid[0][p], mid[1][p], laps[0][p], laps[1][p], du[p]) for p in range(4)]
    return [[b[s] for b in both] for s in range(2)]


def coarse_rate(low, mid, high, du):
    laps = []
    for s in range(2):
        c = mid[s]
        xs = pltpu.roll(c, 1, 0) + pltpu.roll(c, 15, 0)
        ys = pltpu.roll(c, 1, 1) + pltpu.roll(c, 127, 1)
        laps.append((low[s] + high[s]) + 0.25 * (xs + ys) - 3.0 * c)
    return react(mid[0], mid[1], laps[0], laps[1], du)


def average(parts):
    return 0.25 * ((parts[0] + parts[1]) + (parts[2] + parts[3]))


def loop(count, body, chunk=1):
    def many(k, carry):
        for i in range(chunk):
            body(k * chunk + i)
        return carry

    lax.fori_loop(0, count // chunk, many, 0)


def swap(forward):
    rows = lax.broadcasted_iota(jnp.int32, (256, 256), 0)
    cols = lax.broadcasted_iota(jnp.int32, (256, 256), 1)
    if not forward:
        rows, cols = cols, rows
    return jnp.where(rows == 2 * (cols % 128) + cols // 128, 1.0, 0.0).astype(F32)


def kernel(
    init, diff, out, xin, din, tmp, woven, a0, a1, a2, ap, du, cd, v0, v1, r0, r1, r2, own, base, one, two,
    d8, d6, d4, d2, d0, b10, b8, b6, b4, b2, b0, w8, w6, w4, w2, w0, dummy,
    in_sem, near_s, near_r, diff_s, diff_r, cd_s, cd_r, far_s, far_r, prev_s, prev_r, const_s, const_r, state_s, state_r, give_s, give_r,
):
    tm = lax.axis_index("tm")
    gz = lax.axis_index("gz")
    count = lax.axis_size("gz")
    const = {8: d8, 6: d6, 4: d4, 2: d2, 0: d0}
    state = {10: b10, 8: b8, 6: b6, 4: b4, 2: b2, 0: b0}
    middle = {8: w8, 6: w6, 4: w4, 2: w2, 0: w0}

    def at(t, j):
        return {"tm": t, "gz": lax.rem(gz + (j + count), count)}

    def send(src, dst, ssem, rsem, t, j):
        pltpu.make_async_remote_copy(
            src_ref=src, dst_ref=dst, send_sem=ssem, recv_sem=rsem, device_id=at(t, j), device_id_type=MESH
        ).start()

    def wait(sem, units):
        ref = dummy.at[pl.ds(0, units)]
        pltpu.make_async_copy(ref, ref, sem).wait()

    def on(*slices):
        cond = tm == slices[0]
        for t in slices[1:]:
            cond = cond | (tm == t)
        return pl.when(cond)

    load_x = pltpu.make_async_copy(init.at[0], xin, in_sem.at[0])
    load_d = pltpu.make_async_copy(diff, din, in_sem.at[1])
    load_x.start()
    load_d.start()
    barrier = pltpu.get_barrier_semaphore()
    met = pairs()
    for t in range(8):
        @on(t)
        def _(t=t):
            for src, dst, j in met:
                if dst == t:
                    pl.semaphore_signal(barrier, inc=1, device_id=at(src, -j), device_id_type=MESH)

    order = swap(True)
    load_x.wait()
    load_d.wait()

    def split(rows):
        return jnp.dot(rows, order, precision=lax.Precision.HIGHEST, preferred_element_type=F32)

    mixed = split(xin[...].reshape(128, 256)).reshape(4, 32, 256)
    mixed_d = split(din[...].reshape(64, 256)).reshape(2, 32, 256)
    for half in range(2):
        tmp[half, 0:4] = mixed[:, :, half * 128 : half * 128 + 128]
        tmp[half, 4:6] = mixed_d[:, :, half * 128 : half * 128 + 128]
    for layer in range(2):
        for p in range(4):
            rows = pl.ds(p // 2, 16, stride=2)
            for s in range(2):
                a0[3 + layer, s, p] = tmp[p % 2, s * 2 + layer, rows, :]
            du[2 + layer, p] = 0.16 * tmp[p % 2, 4 + layer, rows, :]

    greetings = sum(jnp.where(tm == t, sum(src == t for src, _, _ in met), 0) for t in range(8))
    pl.semaphore_wait(barrier, greetings)

    odd = lax.rem(tm, 2)
    turn = 1 - 2 * odd
    side = pl.ds(4 * odd, 2)
    send(a0.at[4], a0.at[2], near_s.at[0], near_r.at[0], tm, 1)
    send(a0.at[3], a0.at[5], near_s.at[1], near_r.at[1], tm, -1)
    send(du.at[pl.ds(2, 2)], du.at[side], diff_s.at[0], diff_r.at[0], tm, turn)
    send(a0.at[3], a0.at[1], near_s.at[2], near_r.at[2], tm, 1)
    send(a0.at[4], a0.at[6], near_s.at[3], near_r.at[3], tm, -1)
    wait(near_r.at[0], 4)
    send(a0.at[2], a0.at[0], near_s.at[4], near_r.at[4], tm, 1)
    wait(near_r.at[1], 4)
    send(a0.at[5], a0.at[7], near_s.at[5], near_r.at[5], tm, -1)
    wait(diff_r.at[0], 4)
    send(du.at[side], du.at[side], diff_s.at[1], diff_r.at[1], tm + turn, 0)
    wait(diff_r.at[1], 4)
    for i in range(6):
        cd[MID - 2 + i] = average([du[i, p] for p in range(4)])

    def spread(slices):
        for t in slices:
            @on(t)
            def _(t=t):
                for j in sides(COARSE_REACH[t]):
                    if abs(j) > 1:
                        send(cd.at[pl.ds(MID, 2)], cd.at[pl.ds(MID - 2 * j, 2)], cd_s, cd_r, t, j)

    spread((0, 3))
    wait(near_r.at[2], 4)
    wait(near_r.at[3], 4)

    def first(i):
        c = get(a0, i + 1)
        f = fine_rate(get(a0, i), c, get(a0, i + 2), [du[i, p] for p in range(4)])
        for s in range(2):
            for p in range(4):
                a1[i, s, p] = c[s][p] + STEP * f[s][p]
            r0[i, s] = average(f[s])
            v0[i, s] = average(c[s])

    loop(4, lambda i: first(i + 1))

    def second(i):
        c = get(a1, i + 1)
        f = fine_rate(get(a1, i), c, get(a1, i + 2), [du[i + 1, p] for p in range(4)])
        for s in range(2):
            for p in range(4):
                a2[i + 1, s, p] = c[s][p] + STEP * f[s][p]
            r1[i, s] = average(f[s])
            v1[i + 1, s] = average(c[s])

    loop(2, lambda i: second(i + 1))
    wait(near_r.at[4], 4)
    wait(near_r.at[5], 4)
    loop(2, lambda i: first(5 * i))
    loop(2, lambda i: second(3 * i))

    def third(i):
        f = fine_rate(get(a2, i + 1), get(a2, i + 2), get(a2, i + 3), [du[i + 2, p] for p in range(4)])
        for s in range(2):
            r2[i, s] = average(f[s])

    loop(2, third)

    is_first = jnp.where(tm == 0, 1.0, 0.0).astype(F32)
    for i in range(2):
        g_zero = coarse_rate(get_coarse(v0, i + 1), get_coarse(v0, i + 2), get_coarse(v0, i + 3), cd[MID + i])
        g_one = coarse_rate(get_coarse(v1, i + 1), get_coarse(v1, i + 2), get_coarse(v1, i + 3), cd[MID + i])
        for s in range(2):
            rates = (r0[i + 2, s], r1[i + 1, s], r2[i, s])
            c_zero = W_ONE[0] * rates[0] + W_ONE[1] * rates[1] + W_ONE[2] * rates[2]
            c_one = W_TWO[0] * rates[0] + W_TWO[1] * rates[1] + W_TWO[2] * rates[2]
            own[i, 0, s] = c_zero + is_first * v0[i + 2, s] - (1.0 - is_first) * (STEP * g_zero[s])
            own[i, 1, s] = c_one - STEP * g_one[s]

    def share():
        for k, (src, dst, h) in enumerate(CONSTS):
            @on(src)
            def _(k=k, src=src, dst=dst, h=h):
                ref = const[h]
                sems = (const_s.at[k], const_r.at[h // 2])
                for j in reversed(span(h // 2)):
                    here = pl.ds(h + 1 - 2 * j, 2)
                    if src == dst and j == 0:
                        ref[here] = own[...]
                    else:
                        send(own, ref.at[here], *sems, dst, j)
                j = h // 2 + 1
                send(own.at[1, 0], ref.at[0, 0], *sems, dst, j)
                send(own.at[0, 0], ref.at[2 * h + 3, 0], *sems, dst, -j)

    spread((5, 7))
    share()
    send(a2.at[2], a2.at[0], far_s, far_r, tm, 1)
    send(a2.at[3], a2.at[5], far_s, far_r, tm, -1)

    def pass_on():
        wait(far_r, 8)

        @pl.when(tm < 7)
        def _():
            send(a2, ap, prev_s, prev_r, tm + 1, 0)

    @pl.when(tm > 0)
    def _():
        pass_on()

    def prepare():
        @pl.when(tm > 0)
        def _():
            wait(prev_r, 24)

        def body(i):
            for k, (ref, shift) in enumerate(((a0, 1), (a1, 0), (a2, 0), (ap, 0))):
                c = get(ref, i + shift)
                for s in range(2):
                    v = average(c[s])
                    for p in range(4):
                        base[k, i, s, p] = c[s][p] - v

        def body_first(i):
            for k, (ref, shift) in enumerate(((a0, 1), (a1, 0), (a2, 0))):
                c = get(ref, i + shift)
                for s in range(2):
                    v = average(c[s])
                    for p in range(4):
                        base[k, i, s, p] = c[s][p] - v

        @pl.when(tm > 0)
        def _():
            loop(6, body)

        @pl.when(tm == 0)
        def _():
            loop(6, body_first)

    @pl.when(tm > 0)
    def _():
        prepare()

    for t, reach in COARSE_REACH.items():
        @on(t)
        def _(reach=reach):
            wait(cd_r, 2 * reach - 2)

    @on(3)
    def _():
        wait(state_r, 10)

    @on(5)
    def _():
        wait(state_r, 14)

    @on(7)
    def _():
        wait(state_r, 22)

    chunks = {20: 4, 18: 6, 16: 4, 14: 7, 12: 4, 10: 5, 8: 4, 6: 6, 4: 4, 2: 2}

    for h in WIDTHS:
        begin, mid, end, e = state[h + 2], middle[h], state[h], const[h]

        @on(*RUNS[h])
        def _(h=h, begin=begin, mid=mid, end=end, e=e):
            for src, dst, width in CONSTS:
                if width == h:
                    @on(dst)
                    def _(src=src, dst=dst):
                        wait(const_r.at[h // 2], 4 * h + 6 - (4 if src == dst else 0))

            def half(i):
                g = coarse_rate(get_coarse(begin, i), get_coarse(begin, i + 1), get_coarse(begin, i + 2), cd[MID + i - h - 1])
                for s in range(2):
                    mid[i, s] = begin[i + 1, s] + STEP * g[s] + e[i, 0, s]

            def given(i):
                for s in range(2):
                    mid[i, s] = e[i, 0, s]

            def full(i):
                g = coarse_rate(get_coarse(mid, i), get_coarse(mid, i + 1), get_coarse(mid, i + 2), cd[MID + i - h])
                for s in range(2):
                    end[i, s] = mid[i + 1, s] + STEP * g[s] + e[i + 1, 1, s]

            if h == 6:
                @pl.when(tm == 0)
                def _():
                    loop(2 * h + 4, given, 4)

                @pl.when(tm > 0)
                def _():
                    loop(2 * h + 4, half, chunks[2 * h + 4])
            else:
                loop(2 * h + 4, half, chunks[2 * h + 4])
            loop(2 * h + 2, full, chunks[2 * h + 2])

        def give(dst):
            for k, (src_ref, start, dst_ref, to) in enumerate(
                ((state[h + 2], h, b4, 2), (middle[h], h - 1, w2, 1), (state[h], h - 2, b2, 0))
            ):
                send(src_ref.at[pl.ds(start, 6)], dst_ref.at[pl.ds(to, 6)], give_s, give_r, dst, 0)

        if h == 4:
            @on(0)
            def _():
                give(1)

            @on(5, 7)
            def _():
                give(tm - 1)

        if h == 2:
            @on(0)
            def _():
                for j in span(2):
                    send(b2.at[pl.ds(2, 2)], b4.at[pl.ds(4 - 2 * j, 2)], state_s, state_r, 3, j)

        if h == 0:
            @on(0)
            def _():
                for j in reversed(span(5)):
                    send(b0, b10.at[pl.ds(10 - 2 * j, 2)], state_s, state_r, 7, j)
                for j in reversed(span(3)):
                    send(b0, b6.at[pl.ds(6 - 2 * j, 2)], state_s, state_r, 5, j)
                wait(give_s, 18)
                for src_ref, start in ((b4, 2), (w2, 1), (b2, 0)):
                    send(src_ref.at[pl.ds(start, 6)], src_ref.at[pl.ds(start, 6)], give_s, give_r, 2, 0)

    @pl.when(tm == 0)
    def _():
        pass_on()
        prepare()

    @on(1, 2, 4, 6)
    def _():
        wait(give_r, 18)

    def correct(zero, zero_at, one_ref, one_at, two_ref, two_at, start):
        def body(i):
            for k, (ref, shift) in enumerate(((zero, zero_at), (one_ref, one_at), (two_ref, two_at))):
                for s in range(2):
                    w = ref[i + shift, s]
                    for p in range(4):
                        base[k, i, s, p] = base[k, i, s, p] + w
                        if k == 0:
                            if start:
                                base[3, i, s, p] = a0[i + 1, s, p]
                            else:
                                base[3, i, s, p] = base[3, i, s, p] + w

        loop(6, body)

    @pl.when(tm == 0)
    def _():
        correct(v0, 0, w6, 5, b6, 4, True)

    @pl.when(tm > 0)
    def _():
        correct(b4, 2, w2, 1, b2, 0, False)

    def fourth(i):
        d = [du[i + 1, p] for p in range(4)]
        f = [fine_rate(get(base, k, i), get(base, k, i + 1), get(base, k, i + 2), d) for k in range(4)]
        for s in range(2):
            for p in range(4):
                rates = [f[k][s][p] for k in range(3)]
                i_one = W_ONE[0] * rates[0] + W_ONE[1] * rates[1] + W_ONE[2] * rates[2]
                i_two = W_TWO[0] * rates[0] + W_TWO[1] * rates[1] + W_TWO[2] * rates[2]
                b_one = base[3, i + 1, s, p] + STEP * (f[3][s][p] - rates[0]) + i_one
                one[i, s, p] = b_one
                two[i, s, p] = b_one - STEP * rates[1] + i_two

    loop(4, fourth)

    def fifth(i):
        f = fine_rate(get(one, i), get(one, i + 1), get(one, i + 2), [du[i + 2, p] for p in range(4)])
        for s in range(2):
            for p in range(4):
                two[i + 1, s, p] = two[i + 1, s, p] + STEP * f[s][p]

    loop(2, fifth)

    back = swap(False)
    for node, (ref, shift) in enumerate(((base.at[3], 2), (one, 1), (two, 1))):
        rows = []
        for s in range(2):
            for layer in range(2):
                for half in range(2):
                    rows.append(
                        jnp.concatenate([ref[shift + layer, s, 2 * half], ref[shift + layer, s, 2 * half + 1]], axis=1)
                    )
        whole = jnp.dot(jnp.concatenate(rows, 0), back, precision=lax.Precision.HIGHEST, preferred_element_type=F32)
        for s in range(2):
            for layer in range(2):
                for side in range(2):
                    lanes = slice(side * 128, side * 128 + 128)
                    for half in range(2):
                        k = (s * 2 + layer) * 2 + half
                        woven[node, s, layer, side, pl.ds(half, 16, stride=2), :] = whole[k * 16 : k * 16 + 16, lanes]
                    out[0, node, s, layer, :, lanes] = woven[node, s, layer, side]

    for k in range(6):
        wait(near_s.at[k], 4)
    for k in range(2):
        wait(diff_s.at[k], 4)
    wait(far_s, 8)
    for t, reach in COARSE_REACH.items():
        @on(t)
        def _(reach=reach):
            wait(cd_s, 2 * reach - 2)

    @pl.when(tm < 7)
    def _():
        wait(prev_s, 24)

    for k, (src, dst, h) in enumerate(CONSTS):
        @on(src)
        def _(k=k, src=src, dst=dst, h=h):
            wait(const_s.at[k], 4 * h + 6 - (4 if src == dst else 0))

    @on(0)
    def _():
        wait(state_s, 46)

    @on(0, 5, 7)
    def _():
        wait(give_s, 18)


def local(init_states, diffusivity):
    fine = (2, 4, 16, 128)
    coarse = (2, 16, 128)

    def vm(*shape):
        return pltpu.VMEM(shape, F32)

    scratch = [vm(2, 2, 32, 256), vm(2, 32, 256), vm(2, 6, 32, 128), vm(3, 2, 2, 2, 32, 128)]
    scratch += [vm(8, *fine), vm(6, *fine), vm(6, *fine), vm(6, *fine), vm(6, 4, 16, 128), vm(2 * MID + 2, 16, 128)]
    scratch += [vm(6, *coarse), vm(6, *coarse), vm(6, *coarse), vm(4, *coarse), vm(2, *coarse), vm(2, 2, *coarse)]
    scratch += [vm(4, 6, *fine), vm(4, *fine), vm(4, *fine)]
    scratch += [vm(2 * h + 4, 2, *coarse) for h in WIDTHS]
    scratch += [vm(2 * h + 2, *coarse) for h in (10,) + WIDTHS]
    scratch += [vm(2 * h + 4, *coarse) for h in WIDTHS]
    scratch += [vm(48, *coarse)]
    dma = pltpu.SemaphoreType.DMA
    one = [dma(()), dma(())]
    scratch += [dma((2,)), dma((6,)), dma((6,)), dma((2,)), dma((2,))] + one * 3 + [dma((len(CONSTS),)), dma((5,))] + one * 2
    return pl.pallas_call(
        kernel,
        out_shape=jax.ShapeDtypeStruct((1, 3, 2, 2, 32, 256), F32),
        in_specs=[pl.BlockSpec(memory_space=pltpu.HBM)] * 2,
        out_specs=pl.BlockSpec(memory_space=pltpu.VMEM),
        scratch_shapes=scratch,
        name="pfasst",
        compiler_params=pltpu.CompilerParams(
            collective_id=0, has_side_effects=True, vmem_limit_bytes=32 * 1024 * 1024
        ),
    )(init_states, diffusivity)


def solution(mesh):
    placed = (P("tm", None, "gz", None, None), P("gz", None, None))
    return jax.shard_map(
        local,
        mesh=mesh,
        in_specs=placed,
        out_specs=P("tm", None, None, "gz", None, None),
        check_vma=False,
    )
```

```python
import jax
import jax.numpy as jnp
from jax import lax
from jax.experimental import pallas as pl
from jax.experimental.pallas import tpu as pltpu
from jax.sharding import PartitionSpec as P


MESH = pl.DeviceIdType.MESH
F32 = jnp.float32
STEP = 0.4
W_ONE = (0.8 * 5.0 / 24.0, 0.8 / 3.0, -0.8 / 24.0)
W_TWO = (-0.8 / 24.0, 0.8 / 3.0, 0.8 * 5.0 / 24.0)

CONSTS = (
    (0, 0, 6), (1, 0, 4), (2, 0, 2), (3, 0, 0), (3, 3, 2), (4, 7, 8), (5, 7, 6), (6, 7, 4), (7, 7, 2), (4, 5, 4), (5, 5, 2),
)
WIDTHS = (8, 6, 4, 2, 0)
RUNS = {8: (7,), 6: (0, 7), 4: (0, 5, 7), 2: (0, 3, 5, 7), 0: (0,)}
COARSE_REACH = {0: 3, 3: 2, 5: 3, 7: 5}
MID = 10


def span(k):
    return [0] + [s * i for i in range(1, k + 1) for s in (1, -1)]


def sides(k):
    return span(k)[1:]


def pairs():
    out = set()
    for t in range(8):
        out |= {(t, t, j) for j in sides(1)}
        out.add((t, t ^ 1, 0))
        if t:
            out.add((t - 1, t, 0))
    for t, reach in COARSE_REACH.items():
        out |= {(t, t, j) for j in sides(reach) if abs(j) > 1}
    for src, dst, h in CONSTS:
        out |= {(src, dst, j) for j in span(h // 2 + 1) if src != dst or j}
    out |= {(0, 3, j) for j in span(2)} | {(0, 5, j) for j in span(3)} | {(0, 7, j) for j in span(5)}
    out |= {(0, 1, 0), (0, 2, 0), (5, 4, 0), (7, 6, 0)}
    return sorted(out, key=lambda p: (p[0] != p[1] or abs(p[2]) > 1, p))


def get(ref, *at):
    return [[ref[(*at, s, p)] for p in range(4)] for s in range(2)]


def get_coarse(ref, *at):
    return [ref[(*at, s)] for s in range(2)]


def react(u, v, lap_u, lap_v, du):
    uvv = u * v * v
    return du * lap_u - uvv + 0.035 * (1.0 - u), (0.5 * du) * lap_v + uvv - 0.095 * v


def fine_rate(low, mid, high, du):
    laps = []
    for s in range(2):
        row = []
        for p in range(4):
            across = mid[s][p ^ 2]
            along = mid[s][p ^ 1]
            xs = across + pltpu.roll(across, 15 if p & 2 else 1, 0)
            ys = along + pltpu.roll(along, 127 if p & 1 else 1, 1)
            row.append((low[s][p] + high[s][p]) + (xs + ys) - 6.0 * mid[s][p])
        laps.append(row)
    both = [react(mid[0][p], mid[1][p], laps[0][p], laps[1][p], du[p]) for p in range(4)]
    return [[b[s] for b in both] for s in range(2)]


def coarse_rate(low, mid, high, du):
    laps = []
    for s in range(2):
        c = mid[s]
        xs = pltpu.roll(c, 1, 0) + pltpu.roll(c, 15, 0)
        ys = pltpu.roll(c, 1, 1) + pltpu.roll(c, 127, 1)
        laps.append((low[s] + high[s]) + 0.25 * (xs + ys) - 3.0 * c)
    return react(mid[0], mid[1], laps[0], laps[1], du)


def average(parts):
    return 0.25 * ((parts[0] + parts[1]) + (parts[2] + parts[3]))


def loop(count, body, chunk=1):
    def many(k, carry):
        for i in range(chunk):
            body(k * chunk + i)
        return carry

    lax.fori_loop(0, count // chunk, many, 0)


def swap(forward):
    shape = (256, 128) if forward else (128, 256)
    whole = lax.broadcasted_iota(jnp.int32, shape, 0 if forward else 1)
    twice = 2 * lax.broadcasted_iota(jnp.int32, shape, 1 if forward else 0)
    parts = [jnp.where(whole == twice + p, 1.0, 0.0) for p in range(2)]
    return jnp.concatenate(parts, axis=1 if forward else 0).astype(jnp.bfloat16)


def permute(rows, order):
    total = None
    for k in range(3):
        part = rows.astype(jnp.bfloat16)
        moved = jnp.dot(part, order, preferred_element_type=F32)
        total = moved if total is None else total + moved
        if k < 2:
            rows = rows - part.astype(F32)
    return total


def kernel(
    init, diff, out, xin, din, tmp, woven, a0, a1, a2, ap, du, cd, v0, v1, r0, r1, r2, own, base, one, two,
    d8, d6, d4, d2, d0, b10, b8, b6, b4, b2, b0, w8, w6, w4, w2, w0, dummy,
    in_sem, near_s, near_r, diff_s, diff_r, cd_s, cd_r, far_s, far_r, prev_s, prev_r, const_s, const_r, state_s, state_r, give_s, give_r,
):
    tm = lax.axis_index("tm")
    gz = lax.axis_index("gz")
    count = lax.axis_size("gz")
    const = {8: d8, 6: d6, 4: d4, 2: d2, 0: d0}
    state = {10: b10, 8: b8, 6: b6, 4: b4, 2: b2, 0: b0}
    middle = {8: w8, 6: w6, 4: w4, 2: w2, 0: w0}

    def at(t, j):
        return {"tm": t, "gz": lax.rem(gz + (j + count), count)}

    def send(src, dst, ssem, rsem, t, j):
        pltpu.make_async_remote_copy(
            src_ref=src, dst_ref=dst, send_sem=ssem, recv_sem=rsem, device_id=at(t, j), device_id_type=MESH
        ).start()

    def wait(sem, units):
        ref = dummy.at[pl.ds(0, units)]
        pltpu.make_async_copy(ref, ref, sem).wait()

    def on(*slices):
        cond = tm == slices[0]
        for t in slices[1:]:
            cond = cond | (tm == t)
        return pl.when(cond)

    load_x = pltpu.make_async_copy(init.at[0], xin, in_sem.at[0])
    load_d = pltpu.make_async_copy(diff, din, in_sem.at[1])
    load_x.start()
    load_d.start()
    barrier = pltpu.get_barrier_semaphore()
    met = pairs()
    for t in range(8):
        @on(t)
        def _(t=t):
            for src, dst, j in met:
                if dst == t:
                    pl.semaphore_signal(barrier, inc=1, device_id=at(src, -j), device_id_type=MESH)

    order = swap(True)
    load_x.wait()
    load_d.wait()

    mixed = permute(xin[...].reshape(128, 256), order).reshape(4, 32, 256)
    mixed_d = permute(din[...].reshape(64, 256), order).reshape(2, 32, 256)
    for half in range(2):
        tmp[half, 0:4] = mixed[:, :, half * 128 : half * 128 + 128]
        tmp[half, 4:6] = mixed_d[:, :, half * 128 : half * 128 + 128]
    for layer in range(2):
        for p in range(4):
            rows = pl.ds(p // 2, 16, stride=2)
            for s in range(2):
                a0[3 + layer, s, p] = tmp[p % 2, s * 2 + layer, rows, :]
            du[2 + layer, p] = 0.16 * tmp[p % 2, 4 + layer, rows, :]

    greetings = sum(jnp.where(tm == t, sum(src == t for src, _, _ in met), 0) for t in range(8))
    pl.semaphore_wait(barrier, greetings)

    odd = lax.rem(tm, 2)
    turn = 1 - 2 * odd
    side = pl.ds(4 * odd, 2)
    send(a0.at[4], a0.at[2], near_s.at[0], near_r.at[0], tm, 1)
    send(a0.at[3], a0.at[5], near_s.at[1], near_r.at[1], tm, -1)

    @pl.when(tm < 4)
    def _():
        send(du.at[pl.ds(2, 2)], du.at[side], diff_s.at[0], diff_r.at[0], tm, turn)
        send(a0.at[3], a0.at[1], near_s.at[2], near_r.at[2], tm, 1)
        send(a0.at[4], a0.at[6], near_s.at[3], near_r.at[3], tm, -1)

    wait(near_r.at[0], 4)
    send(a0.at[2], a0.at[0], near_s.at[4], near_r.at[4], tm, 1)

    @pl.when(tm > 3)
    def _():
        send(du.at[pl.ds(2, 2)], du.at[side], diff_s.at[0], diff_r.at[0], tm, turn)
        send(a0.at[3], a0.at[1], near_s.at[2], near_r.at[2], tm, 1)
        send(a0.at[4], a0.at[6], near_s.at[3], near_r.at[3], tm, -1)

    wait(near_r.at[1], 4)
    send(a0.at[5], a0.at[7], near_s.at[5], near_r.at[5], tm, -1)
    wait(diff_r.at[0], 4)
    send(du.at[side], du.at[side], diff_s.at[1], diff_r.at[1], tm + turn, 0)
    wait(diff_r.at[1], 4)
    for i in range(6):
        cd[MID - 2 + i] = average([du[i, p] for p in range(4)])

    def spread(slices):
        for t in slices:
            @on(t)
            def _(t=t):
                for j in sides(COARSE_REACH[t]):
                    if abs(j) > 1:
                        send(cd.at[pl.ds(MID, 2)], cd.at[pl.ds(MID - 2 * j, 2)], cd_s, cd_r, t, j)

    spread((0, 3))
    wait(near_r.at[2], 4)
    wait(near_r.at[3], 4)

    def first(i):
        c = get(a0, i + 1)
        f = fine_rate(get(a0, i), c, get(a0, i + 2), [du[i, p] for p in range(4)])
        for s in range(2):
            for p in range(4):
                a1[i, s, p] = c[s][p] + STEP * f[s][p]
            r0[i, s] = average(f[s])
            v0[i, s] = average(c[s])

    loop(4, lambda i: first(i + 1), 2)

    def second(i):
        c = get(a1, i + 1)
        f = fine_rate(get(a1, i), c, get(a1, i + 2), [du[i + 1, p] for p in range(4)])
        for s in range(2):
            for p in range(4):
                a2[i + 1, s, p] = c[s][p] + STEP * f[s][p]
            r1[i, s] = average(f[s])
            v1[i + 1, s] = average(c[s])

    loop(2, lambda i: second(i + 1), 2)
    wait(near_r.at[4], 4)
    wait(near_r.at[5], 4)
    loop(2, lambda i: first(5 * i), 2)
    loop(2, lambda i: second(3 * i), 2)

    def third(i):
        f = fine_rate(get(a2, i + 1), get(a2, i + 2), get(a2, i + 3), [du[i + 2, p] for p in range(4)])
        for s in range(2):
            r2[i, s] = average(f[s])

    loop(2, third, 2)

    is_first = jnp.where(tm == 0, 1.0, 0.0).astype(F32)
    for i in range(2):
        g_zero = coarse_rate(get_coarse(v0, i + 1), get_coarse(v0, i + 2), get_coarse(v0, i + 3), cd[MID + i])
        g_one = coarse_rate(get_coarse(v1, i + 1), get_coarse(v1, i + 2), get_coarse(v1, i + 3), cd[MID + i])
        for s in range(2):
            rates = (r0[i + 2, s], r1[i + 1, s], r2[i, s])
            c_zero = W_ONE[0] * rates[0] + W_ONE[1] * rates[1] + W_ONE[2] * rates[2]
            c_one = W_TWO[0] * rates[0] + W_TWO[1] * rates[1] + W_TWO[2] * rates[2]
            own[i, 0, s] = c_zero + is_first * v0[i + 2, s] - (1.0 - is_first) * (STEP * g_zero[s])
            own[i, 1, s] = c_one - STEP * g_one[s]

    def share():
        for k, (src, dst, h) in enumerate(CONSTS):
            @on(src)
            def _(k=k, src=src, dst=dst, h=h):
                ref = const[h]
                sems = (const_s.at[k], const_r.at[h // 2])
                for j in reversed(span(h // 2)):
                    here = pl.ds(h + 1 - 2 * j, 2)
                    if src == dst and j == 0:
                        ref[here] = own[...]
                    else:
                        send(own, ref.at[here], *sems, dst, j)
                j = h // 2 + 1
                send(own.at[1, 0], ref.at[0, 0], *sems, dst, j)
                send(own.at[0, 0], ref.at[2 * h + 3, 0], *sems, dst, -j)

    spread((5, 7))
    share()
    send(a2.at[2], a2.at[0], far_s, far_r, tm, 1)
    send(a2.at[3], a2.at[5], far_s, far_r, tm, -1)

    def pass_on():
        wait(far_r, 8)

        @pl.when(tm < 7)
        def _():
            send(a2, ap, prev_s, prev_r, tm + 1, 0)

    @pl.when(tm > 0)
    def _():
        pass_on()

    def prepare():
        @pl.when(tm > 0)
        def _():
            wait(prev_r, 24)

        def body(i):
            for k, (ref, shift) in enumerate(((a0, 1), (a1, 0), (a2, 0), (ap, 0))):
                c = get(ref, i + shift)
                for s in range(2):
                    v = average(c[s])
                    for p in range(4):
                        base[k, i, s, p] = c[s][p] - v

        def body_first(i):
            for k, (ref, shift) in enumerate(((a0, 1), (a1, 0), (a2, 0))):
                c = get(ref, i + shift)
                for s in range(2):
                    v = average(c[s])
                    for p in range(4):
                        base[k, i, s, p] = c[s][p] - v

        @pl.when(tm > 0)
        def _():
            loop(6, body)

        @pl.when(tm == 0)
        def _():
            loop(6, body_first)

    @pl.when(tm > 0)
    def _():
        prepare()

    for t, reach in COARSE_REACH.items():
        @on(t)
        def _(reach=reach):
            wait(cd_r, 2 * reach - 2)

    @on(3)
    def _():
        wait(state_r, 10)

    @on(5)
    def _():
        wait(state_r, 14)

    @on(7)
    def _():
        wait(state_r, 22)

    chunks = {20: 10, 18: 9, 16: 8, 14: 7, 12: 6, 10: 10, 8: 8, 6: 6, 4: 4, 2: 2}

    for h in WIDTHS:
        begin, mid, end, e = state[h + 2], middle[h], state[h], const[h]

        @on(*RUNS[h])
        def _(h=h, begin=begin, mid=mid, end=end, e=e):
            for src, dst, width in CONSTS:
                if width == h:
                    @on(dst)
                    def _(src=src, dst=dst):
                        wait(const_r.at[h // 2], 4 * h + 6 - (4 if src == dst else 0))

            def half(i):
                g = coarse_rate(get_coarse(begin, i), get_coarse(begin, i + 1), get_coarse(begin, i + 2), cd[MID + i - h - 1])
                for s in range(2):
                    mid[i, s] = begin[i + 1, s] + STEP * g[s] + e[i, 0, s]

            def given(i):
                for s in range(2):
                    mid[i, s] = e[i, 0, s]

            def full(i):
                g = coarse_rate(get_coarse(mid, i), get_coarse(mid, i + 1), get_coarse(mid, i + 2), cd[MID + i - h])
                for s in range(2):
                    end[i, s] = mid[i + 1, s] + STEP * g[s] + e[i + 1, 1, s]

            if h == 6:
                @pl.when(tm == 0)
                def _():
                    loop(2 * h + 4, given, 4)

                @pl.when(tm > 0)
                def _():
                    loop(2 * h + 4, half, chunks[2 * h + 4])
            else:
                loop(2 * h + 4, half, chunks[2 * h + 4])
            loop(2 * h + 2, full, chunks[2 * h + 2])

        def give(dst):
            for k, (src_ref, start, dst_ref, to) in enumerate(
                ((state[h + 2], h, b4, 2), (middle[h], h - 1, w2, 1), (state[h], h - 2, b2, 0))
            ):
                send(src_ref.at[pl.ds(start, 6)], dst_ref.at[pl.ds(to, 6)], give_s, give_r, dst, 0)

        if h == 4:
            @on(0)
            def _():
                give(1)

            @on(5, 7)
            def _():
                give(tm - 1)

        if h == 2:
            @on(0)
            def _():
                for j in span(2):
                    send(b2.at[pl.ds(2, 2)], b4.at[pl.ds(4 - 2 * j, 2)], state_s, state_r, 3, j)

        if h == 0:
            @on(0)
            def _():
                for j in reversed(span(5)):
                    send(b0, b10.at[pl.ds(10 - 2 * j, 2)], state_s, state_r, 7, j)
                for j in reversed(span(3)):
                    send(b0, b6.at[pl.ds(6 - 2 * j, 2)], state_s, state_r, 5, j)
                wait(give_s, 18)
                for src_ref, start in ((b4, 2), (w2, 1), (b2, 0)):
                    send(src_ref.at[pl.ds(start, 6)], src_ref.at[pl.ds(start, 6)], give_s, give_r, 2, 0)

    @pl.when(tm == 0)
    def _():
        pass_on()
        prepare()

    @on(1, 2, 4, 6)
    def _():
        wait(give_r, 18)

    def correct(zero, zero_at, one_ref, one_at, two_ref, two_at, start):
        def body(i):
            for k, (ref, shift) in enumerate(((zero, zero_at), (one_ref, one_at), (two_ref, two_at))):
                for s in range(2):
                    w = ref[i + shift, s]
                    for p in range(4):
                        base[k, i, s, p] = base[k, i, s, p] + w
                        if k == 0:
                            if start:
                                base[3, i, s, p] = a0[i + 1, s, p]
                            else:
                                base[3, i, s, p] = base[3, i, s, p] + w

        loop(6, body)

    @pl.when(tm == 0)
    def _():
        correct(v0, 0, w6, 5, b6, 4, True)

    @pl.when(tm > 0)
    def _():
        correct(b4, 2, w2, 1, b2, 0, False)

    def fourth(i):
        d = [du[i + 1, p] for p in range(4)]
        f = [fine_rate(get(base, k, i), get(base, k, i + 1), get(base, k, i + 2), d) for k in range(4)]
        for s in range(2):
            for p in range(4):
                rates = [f[k][s][p] for k in range(3)]
                i_one = W_ONE[0] * rates[0] + W_ONE[1] * rates[1] + W_ONE[2] * rates[2]
                i_two = W_TWO[0] * rates[0] + W_TWO[1] * rates[1] + W_TWO[2] * rates[2]
                b_one = base[3, i + 1, s, p] + STEP * (f[3][s][p] - rates[0]) + i_one
                one[i, s, p] = b_one
                two[i, s, p] = b_one - STEP * rates[1] + i_two

    loop(4, fourth)

    def fifth(i):
        f = fine_rate(get(one, i), get(one, i + 1), get(one, i + 2), [du[i + 2, p] for p in range(4)])
        for s in range(2):
            for p in range(4):
                two[i + 1, s, p] = two[i + 1, s, p] + STEP * f[s][p]

    loop(2, fifth, 2)

    back = swap(False)
    for node, (ref, shift) in enumerate(((base.at[3], 2), (one, 1), (two, 1))):
        rows = []
        for s in range(2):
            for layer in range(2):
                for half in range(2):
                    rows.append(
                        jnp.concatenate([ref[shift + layer, s, 2 * half], ref[shift + layer, s, 2 * half + 1]], axis=1)
                    )
        whole = permute(jnp.concatenate(rows, 0), back)
        for s in range(2):
            for layer in range(2):
                for side in range(2):
                    lanes = slice(side * 128, side * 128 + 128)
                    for half in range(2):
                        k = (s * 2 + layer) * 2 + half
                        woven[node, s, layer, side, pl.ds(half, 16, stride=2), :] = whole[k * 16 : k * 16 + 16, lanes]
                    out[0, node, s, layer, :, lanes] = woven[node, s, layer, side]

    for k in range(6):
        wait(near_s.at[k], 4)
    for k in range(2):
        wait(diff_s.at[k], 4)
    wait(far_s, 8)
    for t, reach in COARSE_REACH.items():
        @on(t)
        def _(reach=reach):
            wait(cd_s, 2 * reach - 2)

    @pl.when(tm < 7)
    def _():
        wait(prev_s, 24)

    for k, (src, dst, h) in enumerate(CONSTS):
        @on(src)
        def _(k=k, src=src, dst=dst, h=h):
            wait(const_s.at[k], 4 * h + 6 - (4 if src == dst else 0))

    @on(0)
    def _():
        wait(state_s, 46)

    @on(0, 5, 7)
    def _():
        wait(give_s, 18)


def local(init_states, diffusivity):
    fine = (2, 4, 16, 128)
    coarse = (2, 16, 128)

    def vm(*shape):
        return pltpu.VMEM(shape, F32)

    scratch = [vm(2, 2, 32, 256), vm(2, 32, 256), vm(2, 6, 32, 128), vm(3, 2, 2, 2, 32, 128)]
    scratch += [vm(8, *fine), vm(6, *fine), vm(6, *fine), vm(6, *fine), vm(6, 4, 16, 128), vm(2 * MID + 2, 16, 128)]
    scratch += [vm(6, *coarse), vm(6, *coarse), vm(6, *coarse), vm(4, *coarse), vm(2, *coarse), vm(2, 2, *coarse)]
    scratch += [vm(4, 6, *fine), vm(4, *fine), vm(4, *fine)]
    scratch += [vm(2 * h + 4, 2, *coarse) for h in WIDTHS]
    scratch += [vm(2 * h + 2, *coarse) for h in (10,) + WIDTHS]
    scratch += [vm(2 * h + 4, *coarse) for h in WIDTHS]
    scratch += [vm(48, *coarse)]
    dma = pltpu.SemaphoreType.DMA
    one = [dma(()), dma(())]
    scratch += [dma((2,)), dma((6,)), dma((6,)), dma((2,)), dma((2,))] + one * 3 + [dma((len(CONSTS),)), dma((5,))] + one * 2
    return pl.pallas_call(
        kernel,
        out_shape=jax.ShapeDtypeStruct((1, 3, 2, 2, 32, 256), F32),
        in_specs=[pl.BlockSpec(memory_space=pltpu.HBM)] * 2,
        out_specs=pl.BlockSpec(memory_space=pltpu.VMEM),
        scratch_shapes=scratch,
        name="pfasst",
        compiler_params=pltpu.CompilerParams(
            collective_id=0, has_side_effects=True, vmem_limit_bytes=32 * 1024 * 1024
        ),
    )(init_states, diffusivity)


def solution(mesh):
    placed = (P("tm", None, "gz", None, None), P("gz", None, None))
    return jax.shard_map(
        local,
        mesh=mesh,
        in_specs=placed,
        out_specs=P("tm", None, None, "gz", None, None),
        check_vma=False,
    )
```

```python
import jax
import jax.numpy as jnp
from jax import lax
from jax.experimental import pallas as pl
from jax.experimental.pallas import tpu as pltpu
from jax.sharding import PartitionSpec as P


MESH = pl.DeviceIdType.MESH
F32 = jnp.float32
STEP = 0.4
W_ONE = (0.8 * 5.0 / 24.0, 0.8 / 3.0, -0.8 / 24.0)
W_TWO = (-0.8 / 24.0, 0.8 / 3.0, 0.8 * 5.0 / 24.0)

CONSTS = (
    (0, 0, 6), (1, 0, 4), (2, 0, 2), (3, 0, 0), (2, 3, 4), (3, 3, 2), (4, 7, 8), (5, 7, 6), (6, 7, 4), (7, 7, 2), (4, 5, 4), (5, 5, 2),
)
WIDTHS = (8, 6, 4, 2, 0)
RUNS = {8: (7,), 6: (0, 7), 4: (0, 3, 5, 7), 2: (0, 3, 5, 7), 0: (0,)}
COARSE_REACH = {0: 3, 3: 3, 5: 3, 7: 5}
MID = 10


def span(k):
    return [0] + [s * i for i in range(1, k + 1) for s in (1, -1)]


def sides(k):
    return span(k)[1:]


def pairs():
    out = set()
    for t in range(8):
        out |= {(t, t, j) for j in sides(1)}
        out.add((t, t ^ 1, 0))
        if t:
            out.add((t - 1, t, 0))
    for t, reach in COARSE_REACH.items():
        out |= {(t, t, j) for j in sides(reach) if abs(j) > 1}
    for src, dst, h in CONSTS:
        out |= {(src, dst, j) for j in span(h // 2 + 1) if src != dst or j}
    out |= {(0, 3, j) for j in span(3)} | {(0, 5, j) for j in span(3)} | {(0, 7, j) for j in span(5)}
    out |= {(0, 1, 0), (3, 2, 0), (5, 4, 0), (7, 6, 0)}
    return sorted(out, key=lambda p: (p[0] != p[1] or abs(p[2]) > 1, p))


def get(ref, *at):
    return [[ref[(*at, s, p)] for p in range(4)] for s in range(2)]


def get_coarse(ref, *at):
    return [ref[(*at, s)] for s in range(2)]


def react(u, v, lap_u, lap_v, du):
    uvv = u * v * v
    return du * lap_u - uvv + 0.035 * (1.0 - u), (0.5 * du) * lap_v + uvv - 0.095 * v


def fine_rate(low, mid, high, du):
    laps = []
    for s in range(2):
        row = []
        for p in range(4):
            across = mid[s][p ^ 2]
            along = mid[s][p ^ 1]
            xs = across + pltpu.roll(across, 15 if p & 2 else 1, 0)
            ys = along + pltpu.roll(along, 127 if p & 1 else 1, 1)
            row.append((low[s][p] + high[s][p]) + (xs + ys) - 6.0 * mid[s][p])
        laps.append(row)
    both = [react(mid[0][p], mid[1][p], laps[0][p], laps[1][p], du[p]) for p in range(4)]
    return [[b[s] for b in both] for s in range(2)]


def coarse_rate(low, mid, high, du):
    laps = []
    for s in range(2):
        c = mid[s]
        xs = pltpu.roll(c, 1, 0) + pltpu.roll(c, 15, 0)
        ys = pltpu.roll(c, 1, 1) + pltpu.roll(c, 127, 1)
        laps.append((low[s] + high[s]) + 0.25 * (xs + ys) - 3.0 * c)
    return react(mid[0], mid[1], laps[0], laps[1], du)


def average(parts):
    return 0.25 * ((parts[0] + parts[1]) + (parts[2] + parts[3]))


def loop(count, body, chunk=1):
    def many(k, carry):
        for i in range(chunk):
            body(k * chunk + i)
        return carry

    lax.fori_loop(0, count // chunk, many, 0)


def swap(forward):
    shape = (256, 128) if forward else (128, 256)
    whole = lax.broadcasted_iota(jnp.int32, shape, 0 if forward else 1)
    twice = 2 * lax.broadcasted_iota(jnp.int32, shape, 1 if forward else 0)
    parts = [jnp.where(whole == twice + p, 1.0, 0.0) for p in range(2)]
    return jnp.concatenate(parts, axis=1 if forward else 0).astype(jnp.bfloat16)


def permute(rows, order):
    total = None
    for k in range(3):
        part = rows.astype(jnp.bfloat16)
        moved = jnp.dot(part, order, preferred_element_type=F32)
        total = moved if total is None else total + moved
        if k < 2:
            rows = rows - part.astype(F32)
    return total


def kernel(
    init, diff, out, xin, din, tmp, woven, result, a0, a1, a2, ap, du, cd, v0, v1, r0, r1, r2, own, base, one, two,
    d8, d6, d4, d2, d0, b10, b8, b6, b4, b2, b0, w8, w6, w4, w2, w0, dummy,
    in_sem, out_sem, near_s, near_r, diff_s, diff_r, cd_s, cd_r, far_s, far_r, prev_s, prev_r, const_s, const_r, state_s, state_r, give_s, give_r,
):
    tm = lax.axis_index("tm")
    gz = lax.axis_index("gz")
    count = lax.axis_size("gz")
    const = {8: d8, 6: d6, 4: d4, 2: d2, 0: d0}
    state = {10: b10, 8: b8, 6: b6, 4: b4, 2: b2, 0: b0}
    middle = {8: w8, 6: w6, 4: w4, 2: w2, 0: w0}

    def at(t, j):
        return {"tm": t, "gz": lax.rem(gz + (j + count), count)}

    def send(src, dst, ssem, rsem, t, j):
        pltpu.make_async_remote_copy(
            src_ref=src, dst_ref=dst, send_sem=ssem, recv_sem=rsem, device_id=at(t, j), device_id_type=MESH
        ).start()

    def wait(sem, units):
        ref = dummy.at[pl.ds(0, units)]
        pltpu.make_async_copy(ref, ref, sem).wait()

    def on(*slices):
        cond = tm == slices[0]
        for t in slices[1:]:
            cond = cond | (tm == t)
        return pl.when(cond)

    load_x = pltpu.make_async_copy(init.at[0], xin, in_sem.at[0])
    load_d = pltpu.make_async_copy(diff, din, in_sem.at[1])
    load_x.start()
    load_d.start()
    barrier = pltpu.get_barrier_semaphore()
    met = pairs()
    for t in range(8):
        @on(t)
        def _(t=t):
            for src, dst, j in met:
                if dst == t:
                    pl.semaphore_signal(barrier, inc=1, device_id=at(src, -j), device_id_type=MESH)

    order = swap(True)
    load_x.wait()
    load_d.wait()

    mixed = permute(xin[...].reshape(128, 256), order).reshape(4, 32, 256)
    mixed_d = permute(din[...].reshape(64, 256), order).reshape(2, 32, 256)
    for half in range(2):
        tmp[half, 0:4] = mixed[:, :, half * 128 : half * 128 + 128]
        tmp[half, 4:6] = mixed_d[:, :, half * 128 : half * 128 + 128]
    for layer in range(2):
        for p in range(4):
            rows = pl.ds(p // 2, 16, stride=2)
            for s in range(2):
                a0[3 + layer, s, p] = tmp[p % 2, s * 2 + layer, rows, :]
            du[2 + layer, p] = 0.16 * tmp[p % 2, 4 + layer, rows, :]

    greetings = sum(jnp.where(tm == t, sum(src == t for src, _, _ in met), 0) for t in range(8))
    pl.semaphore_wait(barrier, greetings)

    odd = lax.rem(tm, 2)
    turn = 1 - 2 * odd
    side = pl.ds(4 * odd, 2)
    send(a0.at[4], a0.at[2], near_s.at[0], near_r.at[0], tm, 1)
    send(a0.at[3], a0.at[5], near_s.at[1], near_r.at[1], tm, -1)

    @pl.when(tm < 4)
    def _():
        send(du.at[pl.ds(2, 2)], du.at[side], diff_s.at[0], diff_r.at[0], tm, turn)
        send(a0.at[3], a0.at[1], near_s.at[2], near_r.at[2], tm, 1)
        send(a0.at[4], a0.at[6], near_s.at[3], near_r.at[3], tm, -1)

    wait(near_r.at[0], 4)
    send(a0.at[2], a0.at[0], near_s.at[4], near_r.at[4], tm, 1)

    @pl.when(tm > 3)
    def _():
        send(du.at[pl.ds(2, 2)], du.at[side], diff_s.at[0], diff_r.at[0], tm, turn)
        send(a0.at[3], a0.at[1], near_s.at[2], near_r.at[2], tm, 1)
        send(a0.at[4], a0.at[6], near_s.at[3], near_r.at[3], tm, -1)

    wait(near_r.at[1], 4)
    send(a0.at[5], a0.at[7], near_s.at[5], near_r.at[5], tm, -1)
    wait(diff_r.at[0], 4)
    send(du.at[side], du.at[side], diff_s.at[1], diff_r.at[1], tm + turn, 0)
    wait(diff_r.at[1], 4)
    for i in range(6):
        cd[MID - 2 + i] = average([du[i, p] for p in range(4)])

    def spread(slices):
        for t in slices:
            @on(t)
            def _(t=t):
                for j in sides(COARSE_REACH[t]):
                    if abs(j) > 1:
                        send(cd.at[pl.ds(MID, 2)], cd.at[pl.ds(MID - 2 * j, 2)], cd_s, cd_r, t, j)

    spread((0, 3))
    wait(near_r.at[2], 4)
    wait(near_r.at[3], 4)

    def first(i):
        c = get(a0, i + 1)
        f = fine_rate(get(a0, i), c, get(a0, i + 2), [du[i, p] for p in range(4)])
        for s in range(2):
            for p in range(4):
                a1[i, s, p] = c[s][p] + STEP * f[s][p]
            r0[i, s] = average(f[s])
            v0[i, s] = average(c[s])

    loop(4, lambda i: first(i + 1), 2)

    def second(i):
        c = get(a1, i + 1)
        f = fine_rate(get(a1, i), c, get(a1, i + 2), [du[i + 1, p] for p in range(4)])
        for s in range(2):
            for p in range(4):
                a2[i + 1, s, p] = c[s][p] + STEP * f[s][p]
            r1[i, s] = average(f[s])
            v1[i + 1, s] = average(c[s])

    loop(2, lambda i: second(i + 1), 2)
    wait(near_r.at[4], 4)
    wait(near_r.at[5], 4)
    loop(2, lambda i: first(5 * i), 2)
    loop(2, lambda i: second(3 * i), 2)

    def third(i):
        f = fine_rate(get(a2, i + 1), get(a2, i + 2), get(a2, i + 3), [du[i + 2, p] for p in range(4)])
        for s in range(2):
            r2[i, s] = average(f[s])

    loop(2, third, 2)

    is_first = jnp.where(tm == 0, 1.0, 0.0).astype(F32)
    for i in range(2):
        g_zero = coarse_rate(get_coarse(v0, i + 1), get_coarse(v0, i + 2), get_coarse(v0, i + 3), cd[MID + i])
        g_one = coarse_rate(get_coarse(v1, i + 1), get_coarse(v1, i + 2), get_coarse(v1, i + 3), cd[MID + i])
        for s in range(2):
            rates = (r0[i + 2, s], r1[i + 1, s], r2[i, s])
            c_zero = W_ONE[0] * rates[0] + W_ONE[1] * rates[1] + W_ONE[2] * rates[2]
            c_one = W_TWO[0] * rates[0] + W_TWO[1] * rates[1] + W_TWO[2] * rates[2]
            own[i, 0, s] = c_zero + is_first * v0[i + 2, s] - (1.0 - is_first) * (STEP * g_zero[s])
            own[i, 1, s] = c_one - STEP * g_one[s]

    def share():
        for k, (src, dst, h) in enumerate(CONSTS):
            @on(src)
            def _(k=k, src=src, dst=dst, h=h):
                ref = const[h]
                sems = (const_s.at[k], const_r.at[h // 2])
                for j in reversed(span(h // 2)):
                    here = pl.ds(h + 1 - 2 * j, 2)
                    if src == dst and j == 0:
                        ref[here] = own[...]
                    else:
                        send(own, ref.at[here], *sems, dst, j)
                j = h // 2 + 1
                send(own.at[1, 0], ref.at[0, 0], *sems, dst, j)
                send(own.at[0, 0], ref.at[2 * h + 3, 0], *sems, dst, -j)

    spread((5, 7))
    share()
    send(a2.at[2], a2.at[0], far_s, far_r, tm, 1)
    send(a2.at[3], a2.at[5], far_s, far_r, tm, -1)

    def pass_on():
        wait(far_r, 8)

        @pl.when(tm < 7)
        def _():
            send(a2, ap, prev_s, prev_r, tm + 1, 0)

    @pl.when(tm > 0)
    def _():
        pass_on()

    def prepare():
        @pl.when(tm > 0)
        def _():
            wait(prev_r, 24)

        def body(i):
            for k, (ref, shift) in enumerate(((a0, 1), (a1, 0), (a2, 0), (ap, 0))):
                c = get(ref, i + shift)
                for s in range(2):
                    v = average(c[s])
                    for p in range(4):
                        base[k, i, s, p] = c[s][p] - v

        def body_first(i):
            for k, (ref, shift) in enumerate(((a0, 1), (a1, 0), (a2, 0))):
                c = get(ref, i + shift)
                for s in range(2):
                    v = average(c[s])
                    for p in range(4):
                        base[k, i, s, p] = c[s][p] - v

        @pl.when(tm > 0)
        def _():
            loop(6, body)

        @pl.when(tm == 0)
        def _():
            loop(6, body_first)

    @pl.when(tm > 0)
    def _():
        prepare()

    for t, reach in COARSE_REACH.items():
        @on(t)
        def _(reach=reach):
            wait(cd_r, 2 * reach - 2)

    @on(3, 5)
    def _():
        wait(state_r, 14)

    @on(7)
    def _():
        wait(state_r, 22)

    chunks = {20: 10, 18: 9, 16: 8, 14: 7, 12: 6, 10: 10, 8: 8, 6: 6, 4: 4, 2: 2}

    for h in WIDTHS:
        begin, mid, end, e = state[h + 2], middle[h], state[h], const[h]

        @on(*RUNS[h])
        def _(h=h, begin=begin, mid=mid, end=end, e=e):
            for src, dst, width in CONSTS:
                if width == h:
                    @on(dst)
                    def _(src=src, dst=dst):
                        wait(const_r.at[h // 2], 4 * h + 6 - (4 if src == dst else 0))

            def half(i):
                g = coarse_rate(get_coarse(begin, i), get_coarse(begin, i + 1), get_coarse(begin, i + 2), cd[MID + i - h - 1])
                for s in range(2):
                    mid[i, s] = begin[i + 1, s] + STEP * g[s] + e[i, 0, s]

            def given(i):
                for s in range(2):
                    mid[i, s] = e[i, 0, s]

            def full(i):
                g = coarse_rate(get_coarse(mid, i), get_coarse(mid, i + 1), get_coarse(mid, i + 2), cd[MID + i - h])
                for s in range(2):
                    end[i, s] = mid[i + 1, s] + STEP * g[s] + e[i + 1, 1, s]

            if h == 6:
                @pl.when(tm == 0)
                def _():
                    loop(2 * h + 4, given, 4)

                @pl.when(tm > 0)
                def _():
                    loop(2 * h + 4, half, chunks[2 * h + 4])
            else:
                loop(2 * h + 4, half, chunks[2 * h + 4])
            loop(2 * h + 2, full, chunks[2 * h + 2])

        def give(dst):
            for k, (src_ref, start, dst_ref, to) in enumerate(
                ((state[h + 2], h, b4, 2), (middle[h], h - 1, w2, 1), (state[h], h - 2, b2, 0))
            ):
                send(src_ref.at[pl.ds(start, 6)], dst_ref.at[pl.ds(to, 6)], give_s, give_r, dst, 0)

        if h == 4:
            @on(0)
            def _():
                give(1)
                for j in reversed(span(3)):
                    send(b4.at[pl.ds(4, 2)], b6.at[pl.ds(6 - 2 * j, 2)], state_s, state_r, 3, j)

            @on(3, 5, 7)
            def _():
                give(tm - 1)

        if h == 0:
            @on(0)
            def _():
                for j in reversed(sides(5)[2:]):
                    send(b0, b10.at[pl.ds(10 - 2 * j, 2)], state_s, state_r, 7, j)
                for j in reversed(span(3)):
                    send(b0, b6.at[pl.ds(6 - 2 * j, 2)], state_s, state_r, 5, j)
                for j in reversed(span(1)):
                    send(b0, b10.at[pl.ds(10 - 2 * j, 2)], state_s, state_r, 7, j)

    @pl.when(tm == 0)
    def _():
        pass_on()
        prepare()

    @on(1, 2, 4, 6)
    def _():
        wait(give_r, 18)

    def correct(zero, zero_at, one_ref, one_at, two_ref, two_at, start):
        def body(i):
            for k, (ref, shift) in enumerate(((zero, zero_at), (one_ref, one_at), (two_ref, two_at))):
                for s in range(2):
                    w = ref[i + shift, s]
                    for p in range(4):
                        base[k, i, s, p] = base[k, i, s, p] + w
                        if k == 0:
                            if start:
                                base[3, i, s, p] = a0[i + 1, s, p]
                            else:
                                base[3, i, s, p] = base[3, i, s, p] + w

        loop(6, body)

    @pl.when(tm == 0)
    def _():
        correct(v0, 0, w6, 5, b6, 4, True)

    @pl.when(tm > 0)
    def _():
        correct(b4, 2, w2, 1, b2, 0, False)

    back = swap(False)

    def emit(node, ref, shift):
        rows = []
        for s in range(2):
            for layer in range(2):
                for half in range(2):
                    rows.append(
                        jnp.concatenate([ref[shift + layer, s, 2 * half], ref[shift + layer, s, 2 * half + 1]], axis=1)
                    )
        whole = permute(jnp.concatenate(rows, 0), back)
        for s in range(2):
            for layer in range(2):
                for side in range(2):
                    lanes = slice(side * 128, side * 128 + 128)
                    for half in range(2):
                        k = (s * 2 + layer) * 2 + half
                        woven[node, s, layer, side, pl.ds(half, 16, stride=2), :] = whole[k * 16 : k * 16 + 16, lanes]
                    result[node, s, layer, :, lanes] = woven[node, s, layer, side]
        pltpu.make_async_copy(result.at[node], out.at[0, node], out_sem.at[node]).start()

    emit(0, base.at[3], 2)

    def fourth(i):
        d = [du[i + 1, p] for p in range(4)]
        f = [fine_rate(get(base, k, i), get(base, k, i + 1), get(base, k, i + 2), d) for k in range(4)]
        for s in range(2):
            for p in range(4):
                rates = [f[k][s][p] for k in range(3)]
                i_one = W_ONE[0] * rates[0] + W_ONE[1] * rates[1] + W_ONE[2] * rates[2]
                i_two = W_TWO[0] * rates[0] + W_TWO[1] * rates[1] + W_TWO[2] * rates[2]
                b_one = base[3, i + 1, s, p] + STEP * (f[3][s][p] - rates[0]) + i_one
                one[i, s, p] = b_one
                two[i, s, p] = b_one - STEP * rates[1] + i_two

    loop(4, fourth)

    emit(1, one, 1)

    def fifth(i):
        f = fine_rate(get(one, i), get(one, i + 1), get(one, i + 2), [du[i + 2, p] for p in range(4)])
        for s in range(2):
            for p in range(4):
                two[i + 1, s, p] = two[i + 1, s, p] + STEP * f[s][p]

    loop(2, fifth, 2)

    emit(2, two, 1)

    for node in range(3):
        pltpu.make_async_copy(result.at[node], out.at[0, node], out_sem.at[node]).wait()
    for k in range(6):
        wait(near_s.at[k], 4)
    for k in range(2):
        wait(diff_s.at[k], 4)
    wait(far_s, 8)
    for t, reach in COARSE_REACH.items():
        @on(t)
        def _(reach=reach):
            wait(cd_s, 2 * reach - 2)

    @pl.when(tm < 7)
    def _():
        wait(prev_s, 24)

    for k, (src, dst, h) in enumerate(CONSTS):
        @on(src)
        def _(k=k, src=src, dst=dst, h=h):
            wait(const_s.at[k], 4 * h + 6 - (4 if src == dst else 0))

    @on(0)
    def _():
        wait(state_s, 50)

    @on(0, 3, 5, 7)
    def _():
        wait(give_s, 18)


def local(init_states, diffusivity):
    fine = (2, 4, 16, 128)
    coarse = (2, 16, 128)

    def vm(*shape):
        return pltpu.VMEM(shape, F32)

    scratch = [vm(2, 2, 32, 256), vm(2, 32, 256), vm(2, 6, 32, 128), vm(3, 2, 2, 2, 32, 128), vm(3, 2, 2, 32, 256)]
    scratch += [vm(8, *fine), vm(6, *fine), vm(6, *fine), vm(6, *fine), vm(6, 4, 16, 128), vm(2 * MID + 2, 16, 128)]
    scratch += [vm(6, *coarse), vm(6, *coarse), vm(6, *coarse), vm(4, *coarse), vm(2, *coarse), vm(2, 2, *coarse)]
    scratch += [vm(4, 6, *fine), vm(4, *fine), vm(4, *fine)]
    scratch += [vm(2 * h + 4, 2, *coarse) for h in WIDTHS]
    scratch += [vm(2 * h + 2, *coarse) for h in (10,) + WIDTHS]
    scratch += [vm(2 * h + 4, *coarse) for h in WIDTHS]
    scratch += [vm(52, *coarse)]
    dma = pltpu.SemaphoreType.DMA
    one = [dma(()), dma(())]
    scratch += [dma((2,)), dma((3,)), dma((6,)), dma((6,)), dma((2,)), dma((2,))] + one * 3 + [dma((len(CONSTS),)), dma((5,))] + one * 2
    return pl.pallas_call(
        kernel,
        out_shape=jax.ShapeDtypeStruct((1, 3, 2, 2, 32, 256), F32),
        in_specs=[pl.BlockSpec(memory_space=pltpu.HBM)] * 2,
        out_specs=pl.BlockSpec(memory_space=pl.ANY),
        scratch_shapes=scratch,
        name="pfasst",
        compiler_params=pltpu.CompilerParams(
            collective_id=0, has_side_effects=True, vmem_limit_bytes=60 * 1024 * 1024
        ),
    )(init_states, diffusivity)


def solution(mesh):
    placed = (P("tm", None, "gz", None, None), P("gz", None, None))
    return jax.shard_map(
        local,
        mesh=mesh,
        in_specs=placed,
        out_specs=P("tm", None, None, "gz", None, None),
        check_vma=False,
    )
```

```python
import jax
import jax.numpy as jnp
from jax import lax
from jax.experimental import pallas as pl
from jax.experimental.pallas import tpu as pltpu
from jax.sharding import PartitionSpec as P


MESH = pl.DeviceIdType.MESH
F32 = jnp.float32
STEP = 0.4
W_ONE = (0.8 * 5.0 / 24.0, 0.8 / 3.0, -0.8 / 24.0)
W_TWO = (-0.8 / 24.0, 0.8 / 3.0, 0.8 * 5.0 / 24.0)

CONSTS = (
    (0, 0, 6), (1, 0, 4), (2, 0, 2), (3, 0, 0), (2, 3, 4), (3, 3, 2), (4, 7, 8), (5, 7, 6), (6, 7, 4), (7, 7, 2), (4, 5, 4), (5, 5, 2),
)
WIDTHS = (8, 6, 4, 2, 0)
RUNS = {8: (7,), 6: (0, 7), 4: (0, 3, 5, 7), 2: (0, 3, 5, 7), 0: (0,)}
COARSE_REACH = {0: 3, 3: 3, 5: 3, 7: 5}
MID = 10


def span(k):
    return [0] + [s * i for i in range(1, k + 1) for s in (1, -1)]


def sides(k):
    return span(k)[1:]


def pairs():
    out = set()
    for t in range(8):
        out |= {(t, t, j) for j in sides(1)}
        out.add((t, t ^ 1, 0))
        if t:
            out.add((t - 1, t, 0))
    for t, reach in COARSE_REACH.items():
        out |= {(t, t, j) for j in sides(reach) if abs(j) > 1}
    for src, dst, h in CONSTS:
        out |= {(src, dst, j) for j in span(h // 2 + 1) if src != dst or j}
    out |= {(0, 3, j) for j in span(3)} | {(0, 5, j) for j in span(3)} | {(0, 7, j) for j in span(5)}
    out |= {(0, 1, 0), (3, 2, 0), (5, 4, 0), (7, 6, 0)}
    return sorted(out, key=lambda p: (p[0] != p[1] or abs(p[2]) > 1, p))


def get(ref, *at):
    return [[ref[(*at, s, p)] for p in range(4)] for s in range(2)]


def get_coarse(ref, *at):
    return [ref[(*at, s)] for s in range(2)]


def react(u, v, lap_u, lap_v, du):
    uvv = u * v * v
    return du * lap_u - uvv + 0.035 * (1.0 - u), (0.5 * du) * lap_v + uvv - 0.095 * v


def fine_rate(low, mid, high, du):
    laps = []
    for s in range(2):
        row = []
        for p in range(4):
            across = mid[s][p ^ 2]
            along = mid[s][p ^ 1]
            xs = across + pltpu.roll(across, 15 if p & 2 else 1, 0)
            ys = along + pltpu.roll(along, 127 if p & 1 else 1, 1)
            row.append((low[s][p] + high[s][p]) + (xs + ys) - 6.0 * mid[s][p])
        laps.append(row)
    both = [react(mid[0][p], mid[1][p], laps[0][p], laps[1][p], du[p]) for p in range(4)]
    return [[b[s] for b in both] for s in range(2)]


def coarse_rate(low, mid, high, du):
    laps = []
    for s in range(2):
        c = mid[s]
        xs = pltpu.roll(c, 1, 0) + pltpu.roll(c, 15, 0)
        ys = pltpu.roll(c, 1, 1) + pltpu.roll(c, 127, 1)
        laps.append((low[s] + high[s]) + 0.25 * (xs + ys) - 3.0 * c)
    return react(mid[0], mid[1], laps[0], laps[1], du)


def average(parts):
    return 0.25 * ((parts[0] + parts[1]) + (parts[2] + parts[3]))


def loop(count, body, chunk=1):
    def many(k, carry):
        for i in range(chunk):
            body(k * chunk + i)
        return carry

    if count == chunk:
        many(0, 0)
    else:
        lax.fori_loop(0, count // chunk, many, 0)


def swap(forward):
    shape = (256, 128) if forward else (128, 256)
    whole = lax.broadcasted_iota(jnp.int32, shape, 0 if forward else 1)
    twice = 2 * lax.broadcasted_iota(jnp.int32, shape, 1 if forward else 0)
    parts = [jnp.where(whole == twice + p, 1.0, 0.0) for p in range(2)]
    return jnp.concatenate(parts, axis=1 if forward else 0).astype(jnp.bfloat16)


def permute(rows, order):
    total = None
    for k in range(3):
        part = rows.astype(jnp.bfloat16)
        moved = jnp.dot(part, order, preferred_element_type=F32)
        total = moved if total is None else total + moved
        if k < 2:
            rows = rows - part.astype(F32)
    return total


def kernel(
    init, diff, out, xin, din, tmp, woven, result, a0, a1, a2, ap, du, cd, v0, v1, r0, r1, r2, own, base, one, two,
    d8, d6, d4, d2, d0, b10, b8, b6, b4, b2, b0, w8, w6, w4, w2, w0, dummy,
    in_sem, out_sem, near_s, near_r, diff_s, diff_r, cd_s, cd_r, far_s, far_r, prev_s, prev_r, const_s, const_r, state_s, state_r, give_s, give_r,
):
    tm = lax.axis_index("tm")
    gz = lax.axis_index("gz")
    count = lax.axis_size("gz")
    const = {8: d8, 6: d6, 4: d4, 2: d2, 0: d0}
    state = {10: b10, 8: b8, 6: b6, 4: b4, 2: b2, 0: b0}
    middle = {8: w8, 6: w6, 4: w4, 2: w2, 0: w0}

    def at(t, j):
        return {"tm": t, "gz": lax.rem(gz + (j + count), count)}

    def send(src, dst, ssem, rsem, t, j):
        pltpu.make_async_remote_copy(
            src_ref=src, dst_ref=dst, send_sem=ssem, recv_sem=rsem, device_id=at(t, j), device_id_type=MESH
        ).start()

    def wait(sem, units):
        ref = dummy.at[pl.ds(0, units)]
        pltpu.make_async_copy(ref, ref, sem).wait()

    def on(*slices):
        cond = tm == slices[0]
        for t in slices[1:]:
            cond = cond | (tm == t)
        return pl.when(cond)

    load_x = pltpu.make_async_copy(init.at[0], xin, in_sem.at[0])
    load_d = pltpu.make_async_copy(diff, din, in_sem.at[1])
    load_x.start()
    load_d.start()
    barrier = pltpu.get_barrier_semaphore()
    met = pairs()
    for t in range(8):
        @on(t)
        def _(t=t):
            for src, dst, j in met:
                if dst == t:
                    pl.semaphore_signal(barrier, inc=1, device_id=at(src, -j), device_id_type=MESH)

    order = swap(True)
    load_x.wait()
    load_d.wait()

    mixed = permute(xin[...].reshape(128, 256), order).reshape(4, 32, 256)
    mixed_d = permute(din[...].reshape(64, 256), order).reshape(2, 32, 256)
    for half in range(2):
        tmp[half, 0:4] = mixed[:, :, half * 128 : half * 128 + 128]
        tmp[half, 4:6] = mixed_d[:, :, half * 128 : half * 128 + 128]
    for layer in range(2):
        for p in range(4):
            rows = pl.ds(p // 2, 16, stride=2)
            for s in range(2):
                a0[3 + layer, s, p] = tmp[p % 2, s * 2 + layer, rows, :]
            du[2 + layer, p] = 0.16 * tmp[p % 2, 4 + layer, rows, :]

    greetings = sum(jnp.where(tm == t, sum(src == t for src, _, _ in met), 0) for t in range(8))
    pl.semaphore_wait(barrier, greetings)

    odd = lax.rem(tm, 2)
    turn = 1 - 2 * odd
    side = pl.ds(4 * odd, 2)
    send(a0.at[4], a0.at[2], near_s.at[0], near_r.at[0], tm, 1)
    send(a0.at[3], a0.at[5], near_s.at[1], near_r.at[1], tm, -1)

    @pl.when(tm < 4)
    def _():
        send(du.at[pl.ds(2, 2)], du.at[side], diff_s.at[0], diff_r.at[0], tm, turn)
        send(a0.at[3], a0.at[1], near_s.at[2], near_r.at[2], tm, 1)
        send(a0.at[4], a0.at[6], near_s.at[3], near_r.at[3], tm, -1)

    wait(near_r.at[0], 4)
    send(a0.at[2], a0.at[0], near_s.at[4], near_r.at[4], tm, 1)

    @pl.when(tm > 3)
    def _():
        send(du.at[pl.ds(2, 2)], du.at[side], diff_s.at[0], diff_r.at[0], tm, turn)
        send(a0.at[3], a0.at[1], near_s.at[2], near_r.at[2], tm, 1)
        send(a0.at[4], a0.at[6], near_s.at[3], near_r.at[3], tm, -1)

    wait(near_r.at[1], 4)
    send(a0.at[5], a0.at[7], near_s.at[5], near_r.at[5], tm, -1)
    wait(diff_r.at[0], 4)
    send(du.at[side], du.at[side], diff_s.at[1], diff_r.at[1], tm + turn, 0)
    wait(diff_r.at[1], 4)
    for i in range(6):
        cd[MID - 2 + i] = average([du[i, p] for p in range(4)])

    def spread(slices):
        for t in slices:
            @on(t)
            def _(t=t):
                for j in sides(COARSE_REACH[t]):
                    if abs(j) > 1:
                        send(cd.at[pl.ds(MID, 2)], cd.at[pl.ds(MID - 2 * j, 2)], cd_s, cd_r, t, j)

    spread((0, 3))
    wait(near_r.at[2], 4)
    wait(near_r.at[3], 4)

    def first(i):
        c = get(a0, i + 1)
        f = fine_rate(get(a0, i), c, get(a0, i + 2), [du[i, p] for p in range(4)])
        for s in range(2):
            for p in range(4):
                a1[i, s, p] = c[s][p] + STEP * f[s][p]
            r0[i, s] = average(f[s])
            v0[i, s] = average(c[s])

    loop(4, lambda i: first(i + 1), 2)

    def second(i):
        c = get(a1, i + 1)
        f = fine_rate(get(a1, i), c, get(a1, i + 2), [du[i + 1, p] for p in range(4)])
        for s in range(2):
            for p in range(4):
                a2[i + 1, s, p] = c[s][p] + STEP * f[s][p]
            r1[i, s] = average(f[s])
            v1[i + 1, s] = average(c[s])

    loop(2, lambda i: second(i + 1), 2)
    wait(near_r.at[4], 4)
    wait(near_r.at[5], 4)
    loop(2, lambda i: first(5 * i), 2)
    loop(2, lambda i: second(3 * i), 2)

    def third(i):
        f = fine_rate(get(a2, i + 1), get(a2, i + 2), get(a2, i + 3), [du[i + 2, p] for p in range(4)])
        for s in range(2):
            r2[i, s] = average(f[s])

    loop(2, third, 2)

    is_first = jnp.where(tm == 0, 1.0, 0.0).astype(F32)
    for i in range(2):
        g_zero = coarse_rate(get_coarse(v0, i + 1), get_coarse(v0, i + 2), get_coarse(v0, i + 3), cd[MID + i])
        g_one = coarse_rate(get_coarse(v1, i + 1), get_coarse(v1, i + 2), get_coarse(v1, i + 3), cd[MID + i])
        for s in range(2):
            rates = (r0[i + 2, s], r1[i + 1, s], r2[i, s])
            c_zero = W_ONE[0] * rates[0] + W_ONE[1] * rates[1] + W_ONE[2] * rates[2]
            c_one = W_TWO[0] * rates[0] + W_TWO[1] * rates[1] + W_TWO[2] * rates[2]
            own[i, 0, s] = c_zero + is_first * v0[i + 2, s] - (1.0 - is_first) * (STEP * g_zero[s])
            own[i, 1, s] = c_one - STEP * g_one[s]

    def share():
        for k, (src, dst, h) in enumerate(CONSTS):
            @on(src)
            def _(k=k, src=src, dst=dst, h=h):
                ref = const[h]
                sems = (const_s.at[k], const_r.at[h // 2])
                for j in reversed(span(h // 2)):
                    here = pl.ds(h + 1 - 2 * j, 2)
                    if src == dst and j == 0:
                        ref[here] = own[...]
                    else:
                        send(own, ref.at[here], *sems, dst, j)
                j = h // 2 + 1
                send(own.at[1, 0], ref.at[0, 0], *sems, dst, j)
                send(own.at[0, 0], ref.at[2 * h + 3, 0], *sems, dst, -j)

    share()
    spread((5, 7))
    send(a2.at[2], a2.at[0], far_s, far_r, tm, 1)
    send(a2.at[3], a2.at[5], far_s, far_r, tm, -1)

    def pass_on():
        wait(far_r, 8)

        @pl.when(tm < 7)
        def _():
            send(a2, ap, prev_s, prev_r, tm + 1, 0)

    @pl.when(tm > 0)
    def _():
        pass_on()

    def prepare():
        @pl.when(tm > 0)
        def _():
            wait(prev_r, 24)

        def body(i):
            for k, (ref, shift) in enumerate(((a0, 1), (a1, 0), (a2, 0), (ap, 0))):
                c = get(ref, i + shift)
                for s in range(2):
                    v = average(c[s])
                    for p in range(4):
                        base[k, i, s, p] = c[s][p] - v

        def body_first(i):
            for k, (ref, shift) in enumerate(((a0, 1), (a1, 0), (a2, 0))):
                c = get(ref, i + shift)
                for s in range(2):
                    v = average(c[s])
                    for p in range(4):
                        base[k, i, s, p] = c[s][p] - v

        @pl.when(tm > 0)
        def _():
            loop(6, body)

        @pl.when(tm == 0)
        def _():
            loop(6, body_first)

    @pl.when(tm > 0)
    def _():
        prepare()

    for t, reach in COARSE_REACH.items():
        @on(t)
        def _(reach=reach):
            wait(cd_r, 2 * reach - 2)

    @on(3, 5)
    def _():
        wait(state_r, 14)

    @on(7)
    def _():
        wait(state_r, 22)

    chunks = {20: 10, 18: 9, 16: 8, 14: 7, 12: 6, 10: 10, 8: 8, 6: 6, 4: 4, 2: 2}

    def give(node, dst):
        src, start, ref, to = ((b6, 4, b4, 2), (w4, 3, w2, 1), (b4, 2, b2, 0))[node]
        send(src.at[pl.ds(start, 6)], ref.at[pl.ds(to, 6)], give_s, give_r, dst, 0)

    for h in WIDTHS:
        begin, mid, end, e = state[h + 2], middle[h], state[h], const[h]

        @on(*RUNS[h])
        def _(h=h, begin=begin, mid=mid, end=end, e=e):
            for src, dst, width in CONSTS:
                if width == h:
                    @on(dst)
                    def _(src=src, dst=dst):
                        wait(const_r.at[h // 2], 4 * h + 6 - (4 if src == dst else 0))

            def half(i):
                g = coarse_rate(get_coarse(begin, i), get_coarse(begin, i + 1), get_coarse(begin, i + 2), cd[MID + i - h - 1])
                for s in range(2):
                    mid[i, s] = begin[i + 1, s] + STEP * g[s] + e[i, 0, s]

            def given(i):
                for s in range(2):
                    mid[i, s] = e[i, 0, s]

            def full(i):
                g = coarse_rate(get_coarse(mid, i), get_coarse(mid, i + 1), get_coarse(mid, i + 2), cd[MID + i - h])
                for s in range(2):
                    end[i, s] = mid[i + 1, s] + STEP * g[s] + e[i + 1, 1, s]

            if h == 6:
                @pl.when(tm == 0)
                def _():
                    loop(2 * h + 4, given, 4)

                @pl.when(tm > 0)
                def _():
                    loop(2 * h + 4, half, chunks[2 * h + 4])
            else:
                loop(2 * h + 4, half, chunks[2 * h + 4])
            if h == 4:
                for node in range(2):
                    @pl.when(tm == 0)
                    def _(node=node):
                        give(node, 1)

                    @pl.when(tm > 0)
                    def _(node=node):
                        give(node, tm - 1)
            loop(2 * h + 2, full, chunks[2 * h + 2])

        if h == 4:
            @on(0)
            def _():
                give(2, 1)
                for j in reversed(span(3)):
                    send(b4.at[pl.ds(4, 2)], b6.at[pl.ds(6 - 2 * j, 2)], state_s, state_r, 3, j)

            @on(3, 5, 7)
            def _():
                give(2, tm - 1)

        if h == 0:
            @on(0)
            def _():
                for j in reversed(sides(5)[2:]):
                    send(b0, b10.at[pl.ds(10 - 2 * j, 2)], state_s, state_r, 7, j)
                for j in reversed(span(3)):
                    send(b0, b6.at[pl.ds(6 - 2 * j, 2)], state_s, state_r, 5, j)
                for j in reversed(span(1)):
                    send(b0, b10.at[pl.ds(10 - 2 * j, 2)], state_s, state_r, 7, j)

    @pl.when(tm == 0)
    def _():
        pass_on()
        prepare()

    @on(1, 2, 4, 6)
    def _():
        wait(give_r, 18)

    def correct(zero, zero_at, one_ref, one_at, two_ref, two_at, start):
        def body(i):
            for k, (ref, shift) in enumerate(((zero, zero_at), (one_ref, one_at), (two_ref, two_at))):
                for s in range(2):
                    w = ref[i + shift, s]
                    for p in range(4):
                        base[k, i, s, p] = base[k, i, s, p] + w
                        if k == 0:
                            if start:
                                base[3, i, s, p] = a0[i + 1, s, p]
                            else:
                                base[3, i, s, p] = base[3, i, s, p] + w

        loop(6, body, 2)

    @pl.when(tm == 0)
    def _():
        correct(v0, 0, w6, 5, b6, 4, True)

    @pl.when(tm > 0)
    def _():
        correct(b4, 2, w2, 1, b2, 0, False)

    back = swap(False)

    def emit(node, ref, shift):
        rows = []
        for s in range(2):
            for layer in range(2):
                for half in range(2):
                    rows.append(
                        jnp.concatenate([ref[shift + layer, s, 2 * half], ref[shift + layer, s, 2 * half + 1]], axis=1)
                    )
        whole = permute(jnp.concatenate(rows, 0), back)
        for s in range(2):
            for layer in range(2):
                for side in range(2):
                    lanes = slice(side * 128, side * 128 + 128)
                    for half in range(2):
                        k = (s * 2 + layer) * 2 + half
                        woven[node, s, layer, side, pl.ds(half, 16, stride=2), :] = whole[k * 16 : k * 16 + 16, lanes]
                    result[node, s, layer, :, lanes] = woven[node, s, layer, side]
        pltpu.make_async_copy(result.at[node], out.at[0, node], out_sem.at[node]).start()

    def fourth(i):
        d = [du[i + 1, p] for p in range(4)]
        f = [fine_rate(get(base, k, i), get(base, k, i + 1), get(base, k, i + 2), d) for k in range(4)]
        for s in range(2):
            for p in range(4):
                rates = [f[k][s][p] for k in range(3)]
                i_one = W_ONE[0] * rates[0] + W_ONE[1] * rates[1] + W_ONE[2] * rates[2]
                i_two = W_TWO[0] * rates[0] + W_TWO[1] * rates[1] + W_TWO[2] * rates[2]
                b_one = base[3, i + 1, s, p] + STEP * (f[3][s][p] - rates[0]) + i_one
                one[i, s, p] = b_one
                two[i, s, p] = b_one - STEP * rates[1] + i_two

    loop(4, fourth, 2)

    def fifth(i):
        f = fine_rate(get(one, i), get(one, i + 1), get(one, i + 2), [du[i + 2, p] for p in range(4)])
        for s in range(2):
            for p in range(4):
                two[i + 1, s, p] = two[i + 1, s, p] + STEP * f[s][p]

    loop(2, fifth, 2)

    emit(0, base.at[3], 2)
    emit(1, one, 1)
    emit(2, two, 1)

    for node in range(3):
        pltpu.make_async_copy(result.at[node], out.at[0, node], out_sem.at[node]).wait()
    for k in range(6):
        wait(near_s.at[k], 4)
    for k in range(2):
        wait(diff_s.at[k], 4)
    wait(far_s, 8)
    for t, reach in COARSE_REACH.items():
        @on(t)
        def _(reach=reach):
            wait(cd_s, 2 * reach - 2)

    @pl.when(tm < 7)
    def _():
        wait(prev_s, 24)

    for k, (src, dst, h) in enumerate(CONSTS):
        @on(src)
        def _(k=k, src=src, dst=dst, h=h):
            wait(const_s.at[k], 4 * h + 6 - (4 if src == dst else 0))

    @on(0)
    def _():
        wait(state_s, 50)

    @on(0, 3, 5, 7)
    def _():
        wait(give_s, 18)


def local(init_states, diffusivity):
    fine = (2, 4, 16, 128)
    coarse = (2, 16, 128)

    def vm(*shape):
        return pltpu.VMEM(shape, F32)

    scratch = [vm(2, 2, 32, 256), vm(2, 32, 256), vm(2, 6, 32, 128), vm(3, 2, 2, 2, 32, 128), vm(3, 2, 2, 32, 256)]
    scratch += [vm(8, *fine), vm(6, *fine), vm(6, *fine), vm(6, *fine), vm(6, 4, 16, 128), vm(2 * MID + 2, 16, 128)]
    scratch += [vm(6, *coarse), vm(6, *coarse), vm(6, *coarse), vm(4, *coarse), vm(2, *coarse), vm(2, 2, *coarse)]
    scratch += [vm(4, 6, *fine), vm(4, *fine), vm(4, *fine)]
    scratch += [vm(2 * h + 4, 2, *coarse) for h in WIDTHS]
    scratch += [vm(2 * h + 2, *coarse) for h in (10,) + WIDTHS]
    scratch += [vm(2 * h + 4, *coarse) for h in WIDTHS]
    scratch += [vm(52, *coarse)]
    dma = pltpu.SemaphoreType.DMA
    one = [dma(()), dma(())]
    scratch += [dma((2,)), dma((3,)), dma((6,)), dma((6,)), dma((2,)), dma((2,))] + one * 3 + [dma((len(CONSTS),)), dma((5,))] + one * 2
    return pl.pallas_call(
        kernel,
        out_shape=jax.ShapeDtypeStruct((1, 3, 2, 2, 32, 256), F32),
        in_specs=[pl.BlockSpec(memory_space=pltpu.HBM)] * 2,
        out_specs=pl.BlockSpec(memory_space=pl.ANY),
        scratch_shapes=scratch,
        name="pfasst",
        compiler_params=pltpu.CompilerParams(
            collective_id=0, has_side_effects=True, vmem_limit_bytes=60 * 1024 * 1024
        ),
    )(init_states, diffusivity)


def solution(mesh):
    placed = (P("tm", None, "gz", None, None), P("gz", None, None))
    return jax.shard_map(
        local,
        mesh=mesh,
        in_specs=placed,
        out_specs=P("tm", None, None, "gz", None, None),
        check_vma=False,
    )
```

```python
import jax
import jax.numpy as jnp
from jax import lax
from jax.experimental import pallas as pl
from jax.experimental.pallas import tpu as pltpu
from jax.sharding import PartitionSpec as P


MESH = pl.DeviceIdType.MESH
F32 = jnp.float32
STEP = 0.4
W_ONE = (0.8 * 5.0 / 24.0, 0.8 / 3.0, -0.8 / 24.0)
W_TWO = (-0.8 / 24.0, 0.8 / 3.0, 0.8 * 5.0 / 24.0)

CONSTS = (
    (0, 0, 6), (1, 0, 4), (2, 0, 2), (3, 0, 0), (2, 3, 4), (3, 3, 2), (4, 7, 8), (5, 7, 6), (6, 7, 4), (7, 7, 2), (4, 5, 4), (5, 5, 2),
)
WIDTHS = (8, 6, 4, 2, 0)
RUNS = {8: (7,), 6: (0, 7), 4: (0, 3, 5, 7), 2: (0, 3, 5, 7), 0: (0,)}
COARSE_REACH = {0: 3, 3: 3, 5: 3, 7: 5}
MID = 10


def span(k):
    return [0] + [s * i for i in range(1, k + 1) for s in (1, -1)]


def sides(k):
    return span(k)[1:]


def pairs():
    out = set()
    for t in range(8):
        out |= {(t, t, j) for j in sides(1)}
        out.add((t, t ^ 1, 0))
        if t:
            out.add((t - 1, t, 0))
    for t, reach in COARSE_REACH.items():
        out |= {(t, t, j) for j in sides(reach) if abs(j) > 1}
    for src, dst, h in CONSTS:
        out |= {(src, dst, j) for j in span(h // 2 + 1) if src != dst or j}
    out |= {(0, 3, j) for j in span(3)} | {(0, 5, j) for j in span(3)} | {(0, 7, j) for j in span(5)}
    out |= {(0, 1, 0), (3, 2, 0), (5, 4, 0), (7, 6, 0)}
    return sorted(out, key=lambda p: (p[0] != p[1] or abs(p[2]) > 1, p))


def get(ref, *at):
    return [[ref[(*at, s, p)] for p in range(4)] for s in range(2)]


def get_coarse(ref, *at):
    return [ref[(*at, s)] for s in range(2)]


def react(u, v, lap_u, lap_v, du):
    uvv = u * v * v
    return du * lap_u - uvv + 0.035 * (1.0 - u), (0.5 * du) * lap_v + uvv - 0.095 * v


def fine_rate(low, mid, high, du):
    laps = []
    for s in range(2):
        row = []
        for p in range(4):
            across = mid[s][p ^ 2]
            along = mid[s][p ^ 1]
            xs = across + pltpu.roll(across, 15 if p & 2 else 1, 0)
            ys = along + pltpu.roll(along, 127 if p & 1 else 1, 1)
            row.append((low[s][p] + high[s][p]) + (xs + ys) - 6.0 * mid[s][p])
        laps.append(row)
    both = [react(mid[0][p], mid[1][p], laps[0][p], laps[1][p], du[p]) for p in range(4)]
    return [[b[s] for b in both] for s in range(2)]


def coarse_rate(low, mid, high, du):
    laps = []
    for s in range(2):
        c = mid[s]
        xs = pltpu.roll(c, 1, 0) + pltpu.roll(c, 15, 0)
        ys = pltpu.roll(c, 1, 1) + pltpu.roll(c, 127, 1)
        laps.append((low[s] + high[s]) + 0.25 * (xs + ys) - 3.0 * c)
    return react(mid[0], mid[1], laps[0], laps[1], du)


def average(parts):
    return 0.25 * ((parts[0] + parts[1]) + (parts[2] + parts[3]))


def loop(count, body, chunk=1):
    def many(k, carry):
        for i in range(chunk):
            body(k * chunk + i)
        return carry

    if count == chunk:
        many(0, 0)
    else:
        lax.fori_loop(0, count // chunk, many, 0)


def swap(forward):
    shape = (256, 128) if forward else (128, 256)
    whole = lax.broadcasted_iota(jnp.int32, shape, 0 if forward else 1)
    twice = 2 * lax.broadcasted_iota(jnp.int32, shape, 1 if forward else 0)
    parts = [jnp.where(whole == twice + p, 1.0, 0.0) for p in range(2)]
    return jnp.concatenate(parts, axis=1 if forward else 0).astype(jnp.bfloat16)


def permute(rows, order):
    total = None
    for k in range(3):
        part = rows.astype(jnp.bfloat16)
        moved = jnp.dot(part, order, preferred_element_type=F32)
        total = moved if total is None else total + moved
        if k < 2:
            rows = rows - part.astype(F32)
    return total


def kernel(
    init, diff, out, xin, din, tmp, woven, result, a0, a1, a2, ap, du, cd, v0, v1, r0, r1, r2, own, base, one, two,
    d8, d6, d4, d2, d0, b10, b8, b6, b4, b2, b0, w8, w6, w4, w2, w0, dummy,
    in_sem, out_sem, near_s, near_r, diff_s, diff_r, cd_s, cd_r, far_s, far_r, prev_s, prev_r, const_s, const_r, state_s, state_r, give_s, give_r,
):
    tm = lax.axis_index("tm")
    gz = lax.axis_index("gz")
    count = lax.axis_size("gz")
    const = {8: d8, 6: d6, 4: d4, 2: d2, 0: d0}
    state = {10: b10, 8: b8, 6: b6, 4: b4, 2: b2, 0: b0}
    middle = {8: w8, 6: w6, 4: w4, 2: w2, 0: w0}

    def at(t, j):
        return {"tm": t, "gz": lax.rem(gz + (j + count), count)}

    def send(src, dst, ssem, rsem, t, j):
        pltpu.make_async_remote_copy(
            src_ref=src, dst_ref=dst, send_sem=ssem, recv_sem=rsem, device_id=at(t, j), device_id_type=MESH
        ).start()

    def wait(sem, units):
        ref = dummy.at[pl.ds(0, units)]
        pltpu.make_async_copy(ref, ref, sem).wait()

    def on(*slices):
        cond = tm == slices[0]
        for t in slices[1:]:
            cond = cond | (tm == t)
        return pl.when(cond)

    load_x = pltpu.make_async_copy(init.at[0], xin, in_sem.at[0])
    load_d = pltpu.make_async_copy(diff, din, in_sem.at[1])
    load_x.start()
    load_d.start()
    barrier = pltpu.get_barrier_semaphore()
    met = pairs()
    for t in range(8):
        @on(t)
        def _(t=t):
            for src, dst, j in met:
                if dst == t:
                    pl.semaphore_signal(barrier, inc=1, device_id=at(src, -j), device_id_type=MESH)

    order = swap(True)
    load_x.wait()
    load_d.wait()

    mixed = permute(xin[...].reshape(128, 256), order).reshape(4, 32, 256)
    mixed_d = permute(din[...].reshape(64, 256), order).reshape(2, 32, 256)
    for half in range(2):
        tmp[half, 0:4] = mixed[:, :, half * 128 : half * 128 + 128]
        tmp[half, 4:6] = mixed_d[:, :, half * 128 : half * 128 + 128]
    for layer in range(2):
        for p in range(4):
            rows = pl.ds(p // 2, 16, stride=2)
            for s in range(2):
                a0[3 + layer, s, p] = tmp[p % 2, s * 2 + layer, rows, :]
            du[2 + layer, p] = 0.16 * tmp[p % 2, 4 + layer, rows, :]

    greetings = sum(jnp.where(tm == t, sum(src == t for src, _, _ in met), 0) for t in range(8))
    pl.semaphore_wait(barrier, greetings)

    odd = lax.rem(tm, 2)
    turn = 1 - 2 * odd
    side = pl.ds(4 * odd, 2)
    send(a0.at[4], a0.at[2], near_s.at[0], near_r.at[0], tm, 1)
    send(a0.at[3], a0.at[5], near_s.at[1], near_r.at[1], tm, -1)

    @pl.when(tm < 4)
    def _():
        send(du.at[pl.ds(2, 2)], du.at[side], diff_s.at[0], diff_r.at[0], tm, turn)
        send(a0.at[3], a0.at[1], near_s.at[2], near_r.at[2], tm, 1)
        send(a0.at[4], a0.at[6], near_s.at[3], near_r.at[3], tm, -1)

    wait(near_r.at[0], 4)
    send(a0.at[2], a0.at[0], near_s.at[4], near_r.at[4], tm, 1)

    @pl.when(tm > 3)
    def _():
        send(du.at[pl.ds(2, 2)], du.at[side], diff_s.at[0], diff_r.at[0], tm, turn)
        send(a0.at[3], a0.at[1], near_s.at[2], near_r.at[2], tm, 1)
        send(a0.at[4], a0.at[6], near_s.at[3], near_r.at[3], tm, -1)

    wait(near_r.at[1], 4)
    send(a0.at[5], a0.at[7], near_s.at[5], near_r.at[5], tm, -1)
    wait(diff_r.at[0], 4)
    send(du.at[side], du.at[side], diff_s.at[1], diff_r.at[1], tm + turn, 0)
    wait(diff_r.at[1], 4)
    for i in range(6):
        cd[MID - 2 + i] = average([du[i, p] for p in range(4)])

    def spread(slices):
        for t in slices:
            @on(t)
            def _(t=t):
                for j in sides(COARSE_REACH[t]):
                    if abs(j) > 1:
                        send(cd.at[pl.ds(MID, 2)], cd.at[pl.ds(MID - 2 * j, 2)], cd_s, cd_r, t, j)

    spread((0, 3))
    wait(near_r.at[2], 4)
    wait(near_r.at[3], 4)

    def first(i):
        c = get(a0, i + 1)
        f = fine_rate(get(a0, i), c, get(a0, i + 2), [du[i, p] for p in range(4)])
        for s in range(2):
            for p in range(4):
                a1[i, s, p] = c[s][p] + STEP * f[s][p]
            r0[i, s] = average(f[s])
            v0[i, s] = average(c[s])

    loop(4, lambda i: first(i + 1), 2)

    def second(i):
        c = get(a1, i + 1)
        f = fine_rate(get(a1, i), c, get(a1, i + 2), [du[i + 1, p] for p in range(4)])
        for s in range(2):
            for p in range(4):
                a2[i + 1, s, p] = c[s][p] + STEP * f[s][p]
            r1[i, s] = average(f[s])
            v1[i + 1, s] = average(c[s])

    loop(2, lambda i: second(i + 1), 2)
    wait(near_r.at[4], 4)
    wait(near_r.at[5], 4)
    loop(2, lambda i: first(5 * i), 2)
    loop(2, lambda i: second(3 * i), 2)

    def third(i):
        f = fine_rate(get(a2, i + 1), get(a2, i + 2), get(a2, i + 3), [du[i + 2, p] for p in range(4)])
        for s in range(2):
            r2[i, s] = average(f[s])

    loop(2, third, 2)

    is_first = jnp.where(tm == 0, 1.0, 0.0).astype(F32)
    for i in range(2):
        g_zero = coarse_rate(get_coarse(v0, i + 1), get_coarse(v0, i + 2), get_coarse(v0, i + 3), cd[MID + i])
        g_one = coarse_rate(get_coarse(v1, i + 1), get_coarse(v1, i + 2), get_coarse(v1, i + 3), cd[MID + i])
        for s in range(2):
            rates = (r0[i + 2, s], r1[i + 1, s], r2[i, s])
            c_zero = W_ONE[0] * rates[0] + W_ONE[1] * rates[1] + W_ONE[2] * rates[2]
            c_one = W_TWO[0] * rates[0] + W_TWO[1] * rates[1] + W_TWO[2] * rates[2]
            own[i, 0, s] = c_zero + is_first * v0[i + 2, s] - (1.0 - is_first) * (STEP * g_zero[s])
            own[i, 1, s] = c_one - STEP * g_one[s]

    def share():
        for k, (src, dst, h) in enumerate(CONSTS):
            @on(src)
            def _(k=k, src=src, dst=dst, h=h):
                ref = const[h]
                sems = (const_s.at[k], const_r.at[h // 2])
                for j in reversed(span(h // 2)):
                    here = pl.ds(h + 1 - 2 * j, 2)
                    if src == dst and j == 0:
                        ref[here] = own[...]
                    else:
                        send(own, ref.at[here], *sems, dst, j)
                j = h // 2 + 1
                send(own.at[1, 0], ref.at[0, 0], *sems, dst, j)
                send(own.at[0, 0], ref.at[2 * h + 3, 0], *sems, dst, -j)

    share()
    spread((5, 7))
    send(a2.at[2], a2.at[0], far_s, far_r, tm, 1)
    send(a2.at[3], a2.at[5], far_s, far_r, tm, -1)

    def pass_on():
        wait(far_r, 8)

        @pl.when(tm < 7)
        def _():
            send(a2, ap, prev_s, prev_r, tm + 1, 0)

    @pl.when(tm > 0)
    def _():
        pass_on()

    def prepare():
        @pl.when(tm > 0)
        def _():
            wait(prev_r, 24)

        def body(i):
            for k, (ref, shift) in enumerate(((a0, 1), (a1, 0), (a2, 0), (ap, 0))):
                c = get(ref, i + shift)
                for s in range(2):
                    v = average(c[s])
                    for p in range(4):
                        base[k, i, s, p] = c[s][p] - v

        def body_first(i):
            for k, (ref, shift) in enumerate(((a0, 1), (a1, 0), (a2, 0))):
                c = get(ref, i + shift)
                for s in range(2):
                    v = average(c[s])
                    for p in range(4):
                        base[k, i, s, p] = c[s][p] - v

        @pl.when(tm > 0)
        def _():
            loop(6, body)

        @pl.when(tm == 0)
        def _():
            loop(6, body_first)

    @pl.when(tm > 0)
    def _():
        prepare()

    for t, reach in COARSE_REACH.items():
        @on(t)
        def _(reach=reach):
            wait(cd_r, 2 * reach - 2)

    @on(3, 5)
    def _():
        wait(state_r, 14)

    @on(7)
    def _():
        wait(state_r, 22)

    chunks = {20: 10, 18: 9, 16: 8, 14: 7, 12: 6, 10: 10, 8: 8, 6: 6, 4: 4, 2: 2}

    def give(node, dst):
        src, start, ref, to = ((b6, 4, b4, 2), (w4, 3, w2, 1), (b4, 2, b2, 0))[node]
        send(src.at[pl.ds(start, 6)], ref.at[pl.ds(to, 6)], give_s, give_r, dst, 0)

    for h in WIDTHS:
        begin, mid, end, e = state[h + 2], middle[h], state[h], const[h]

        @on(*RUNS[h])
        def _(h=h, begin=begin, mid=mid, end=end, e=e):
            for src, dst, width in CONSTS:
                if width == h:
                    @on(dst)
                    def _(src=src, dst=dst):
                        wait(const_r.at[h // 2], 4 * h + 6 - (4 if src == dst else 0))

            def half(i):
                g = coarse_rate(get_coarse(begin, i), get_coarse(begin, i + 1), get_coarse(begin, i + 2), cd[MID + i - h - 1])
                for s in range(2):
                    mid[i, s] = begin[i + 1, s] + STEP * g[s] + e[i, 0, s]

            def given(i):
                for s in range(2):
                    mid[i, s] = e[i, 0, s]

            def full(i):
                g = coarse_rate(get_coarse(mid, i), get_coarse(mid, i + 1), get_coarse(mid, i + 2), cd[MID + i - h])
                for s in range(2):
                    end[i, s] = mid[i + 1, s] + STEP * g[s] + e[i + 1, 1, s]

            if h == 6:
                @pl.when(tm == 0)
                def _():
                    loop(2 * h + 4, given, 4)

                @pl.when(tm > 0)
                def _():
                    loop(2 * h + 4, half, chunks[2 * h + 4])
            else:
                loop(2 * h + 4, half, chunks[2 * h + 4])
            if h == 4:
                for node in range(2):
                    @pl.when(tm == 0)
                    def _(node=node):
                        give(node, 1)

                    @pl.when(tm > 0)
                    def _(node=node):
                        give(node, tm - 1)
            loop(2 * h + 2, full, chunks[2 * h + 2])

        if h == 4:
            @on(0)
            def _():
                give(2, 1)
                for j in reversed(span(3)):
                    send(b4.at[pl.ds(4, 2)], b6.at[pl.ds(6 - 2 * j, 2)], state_s, state_r, 3, j)

            @on(3, 5, 7)
            def _():
                give(2, tm - 1)

        if h == 0:
            @on(0)
            def _():
                for j in reversed(sides(5)[2:]):
                    send(b0, b10.at[pl.ds(10 - 2 * j, 2)], state_s, state_r, 7, j)
                for j in reversed(span(3)):
                    send(b0, b6.at[pl.ds(6 - 2 * j, 2)], state_s, state_r, 5, j)
                for j in reversed(span(1)):
                    send(b0, b10.at[pl.ds(10 - 2 * j, 2)], state_s, state_r, 7, j)

    @pl.when(tm == 0)
    def _():
        pass_on()
        prepare()

    @on(1, 2, 4, 6)
    def _():
        wait(give_r, 18)

    def correct(zero, zero_at, one_ref, one_at, two_ref, two_at, start):
        def body(i):
            for k, (ref, shift) in enumerate(((zero, zero_at), (one_ref, one_at), (two_ref, two_at))):
                for s in range(2):
                    w = ref[i + shift, s]
                    for p in range(4):
                        base[k, i, s, p] = base[k, i, s, p] + w
                        if k == 0:
                            if start:
                                base[3, i, s, p] = a0[i + 1, s, p]
                            else:
                                base[3, i, s, p] = base[3, i, s, p] + w

        loop(6, body, 2)

    @pl.when(tm == 0)
    def _():
        correct(v0, 0, w6, 5, b6, 4, True)

    @pl.when(tm > 0)
    def _():
        correct(b4, 2, w2, 1, b2, 0, False)

    back = swap(False)

    def emit(node, ref, shift):
        rows = []
        for s in range(2):
            for layer in range(2):
                for half in range(2):
                    rows.append(
                        jnp.concatenate([ref[shift + layer, s, 2 * half], ref[shift + layer, s, 2 * half + 1]], axis=1)
                    )
        whole = permute(jnp.concatenate(rows, 0), back)
        for s in range(2):
            for layer in range(2):
                for side in range(2):
                    lanes = slice(side * 128, side * 128 + 128)
                    for half in range(2):
                        k = (s * 2 + layer) * 2 + half
                        woven[node, s, layer, side, pl.ds(half, 16, stride=2), :] = whole[k * 16 : k * 16 + 16, lanes]
                    result[node, s, layer, :, lanes] = woven[node, s, layer, side]
        pltpu.make_async_copy(result.at[node], out.at[0, node], out_sem.at[node]).start()

    def fourth(i):
        d = [du[i + 1, p] for p in range(4)]
        f = [fine_rate(get(base, k, i), get(base, k, i + 1), get(base, k, i + 2), d) for k in range(4)]
        for s in range(2):
            for p in range(4):
                rates = [f[k][s][p] for k in range(3)]
                i_one = W_ONE[0] * rates[0] + W_ONE[1] * rates[1] + W_ONE[2] * rates[2]
                i_two = W_TWO[0] * rates[0] + W_TWO[1] * rates[1] + W_TWO[2] * rates[2]
                b_one = base[3, i + 1, s, p] + STEP * (f[3][s][p] - rates[0]) + i_one
                one[i, s, p] = b_one
                two[i, s, p] = b_one - STEP * rates[1] + i_two

    loop(4, fourth, 4)

    def fifth(i):
        f = fine_rate(get(one, i), get(one, i + 1), get(one, i + 2), [du[i + 2, p] for p in range(4)])
        for s in range(2):
            for p in range(4):
                two[i + 1, s, p] = two[i + 1, s, p] + STEP * f[s][p]

    loop(2, fifth, 2)

    emit(0, base.at[3], 2)
    emit(1, one, 1)
    emit(2, two, 1)

    for node in range(3):
        pltpu.make_async_copy(result.at[node], out.at[0, node], out_sem.at[node]).wait()
    for k in range(6):
        wait(near_s.at[k], 4)
    for k in range(2):
        wait(diff_s.at[k], 4)
    wait(far_s, 8)
    for t, reach in COARSE_REACH.items():
        @on(t)
        def _(reach=reach):
            wait(cd_s, 2 * reach - 2)

    @pl.when(tm < 7)
    def _():
        wait(prev_s, 24)

    for k, (src, dst, h) in enumerate(CONSTS):
        @on(src)
        def _(k=k, src=src, dst=dst, h=h):
            wait(const_s.at[k], 4 * h + 6 - (4 if src == dst else 0))

    @on(0)
    def _():
        wait(state_s, 50)

    @on(0, 3, 5, 7)
    def _():
        wait(give_s, 18)


def local(init_states, diffusivity):
    fine = (2, 4, 16, 128)
    coarse = (2, 16, 128)

    def vm(*shape):
        return pltpu.VMEM(shape, F32)

    scratch = [vm(2, 2, 32, 256), vm(2, 32, 256), vm(2, 6, 32, 128), vm(3, 2, 2, 2, 32, 128), vm(3, 2, 2, 32, 256)]
    scratch += [vm(8, *fine), vm(6, *fine), vm(6, *fine), vm(6, *fine), vm(6, 4, 16, 128), vm(2 * MID + 2, 16, 128)]
    scratch += [vm(6, *coarse), vm(6, *coarse), vm(6, *coarse), vm(4, *coarse), vm(2, *coarse), vm(2, 2, *coarse)]
    scratch += [vm(4, 6, *fine), vm(4, *fine), vm(4, *fine)]
    scratch += [vm(2 * h + 4, 2, *coarse) for h in WIDTHS]
    scratch += [vm(2 * h + 2, *coarse) for h in (10,) + WIDTHS]
    scratch += [vm(2 * h + 4, *coarse) for h in WIDTHS]
    scratch += [vm(52, *coarse)]
    dma = pltpu.SemaphoreType.DMA
    one = [dma(()), dma(())]
    scratch += [dma((2,)), dma((3,)), dma((6,)), dma((6,)), dma((2,)), dma((2,))] + one * 3 + [dma((len(CONSTS),)), dma((5,))] + one * 2
    return pl.pallas_call(
        kernel,
        out_shape=jax.ShapeDtypeStruct((1, 3, 2, 2, 32, 256), F32),
        in_specs=[pl.BlockSpec(memory_space=pltpu.HBM)] * 2,
        out_specs=pl.BlockSpec(memory_space=pl.ANY),
        scratch_shapes=scratch,
        name="pfasst",
        compiler_params=pltpu.CompilerParams(
            collective_id=0, has_side_effects=True, vmem_limit_bytes=60 * 1024 * 1024
        ),
    )(init_states, diffusivity)


def solution(mesh):
    placed = (P("tm", None, "gz", None, None), P("gz", None, None))
    return jax.shard_map(
        local,
        mesh=mesh,
        in_specs=placed,
        out_specs=P("tm", None, None, "gz", None, None),
        check_vma=False,
    )
```
